128 devices in a mesh: dp: 16 (over y, z), ctx: 8 (over x, core).
Axes of the slice: x: 4, y: 4, z: 4, core: 2. Of those that a mesh axis runs over, the one named last changes fastest.
Arguments:
- hidden: bfloat16 [16, 4096, 3584], P('dp', 'ctx'), may hold values from -20 to 20, as said below
- w_qkv: bfloat16 [3584, 2304], P(('dp', 'ctx')), may hold values from -0.09375 to 0.09375
- bias_qkv: bfloat16 [2304], replicated, may hold values from -3 to 3
- doc_lengths: int32 [16, 16], P('dp'), may hold values from 1 to 2048, 4096 in all within a row
- span_order: int32 [16, 8], P('dp'), may hold values from 0 to 7, each once within a row
Outputs:
- attended: bfloat16 [16, 4096, 1792], P('dp', 'ctx')
The draws below stay inside these ranges and needn't reach their ends.
Inputs may be any that keep to these rules, and one draw needn't show every extreme that they name: `hidden`: order one in most rows. `span_order`: each group's row is a permutation of 0 to 7.
All inputs are finite; a program needn't handle non-finite values.
Results may differ from the reference program's by a relative error of at most 0.012.
The reference program's roundings to bfloat16 on the way count: a program that leaves them out, or rounds other values in their place, can miss the bound.
Values may be sent and summed in bfloat16 or wider, within the bound.
No kernel may reach another device: no remote copies, remote signals or barrier semaphores. Data moves between devices by JAX's collectives and lax.ppermute only.
A program may use at most 256 MiB of HBM per device.

```python
import math
import jax
import jax.numpy as jnp
import numpy as np
from jax import lax

D = 3584
HEADS_Q = 14
KV_HEADS = 2
HEAD_DIM = 128
TOK_DEV = 512
NDOC = 16
COLS = 2304
SEQ = 4096
MAXDOC = 2048
N_DP = 16
N_CTX = 8


def draw_hidden(key, part):
    key = jax.random.fold_in(key, 11)
    shape = (N_DP, SEQ, D)
    return jnp.clip(jax.random.normal(key, shape, jnp.float32), -6.0, 6.0).astype(jnp.bfloat16)


def level_of(own_key, shape, shards, low, largest):
    def one(axis_at, shards_of):
        heights = jax.random.uniform(jax.random.fold_in(jax.random.fold_in(own_key, 6), axis_at), (shards_of,), jnp.float32, low / len(shards), largest / len(shards))
        return jnp.repeat(jnp.exp(heights), shape[axis_at] // shards_of).reshape((-1,) + (1,) * (len(shape) - axis_at - 1))

    level = one(*shards[0])
    for cut in shards[1:]:
        level = level * one(*cut)
    return level


def profile(amount, total, most, skew):
    loads = [(1 << 20) // math.isqrt(grade ** skew) + 1 for grade in range(2, amount + 1)]
    surplus, counts = total - most - (amount - 1), [1] * (amount - 1)
    while surplus > 0:
        free = [i for i in range(amount - 1) if counts[i] < most]
        whole, left = sum([loads[i] for i in free]), surplus
        for i in free:
            addition = min(most - counts[i], max(1, left * loads[i] // whole), surplus)
            counts[i] = counts[i] + addition
            surplus = surplus - addition
    return np.array([most] + counts)


def uneven(stream_key, count, total, bound, slope):
    if count == 2:
        one = jax.random.randint(stream_key, (), max(1, total - bound), min(bound, total - 1) + 1)
        return jnp.stack([one, total - one])
    sizes = jnp.asarray(profile(count, total, bound, slope), jnp.int32)
    twos = (count - 1) // 2
    source_of, sink = sizes[1:1 + 2 * twos:2], sizes[2:2 + 2 * twos:2]
    room = jnp.minimum(source_of - 1, bound - sink)
    moved = jax.random.randint(jax.random.fold_in(stream_key, 1), (twos,), 0, 1 << 20) % (room + 1)
    sizes = sizes.at[1:1 + 2 * twos:2].set(source_of - moved).at[2:2 + 2 * twos:2].set(sink + moved)
    return sizes[jax.random.permutation(jax.random.fold_in(stream_key, 2), count)]


def bell_draw(stream_key, shape, scale, reach, cuts=(), dtype=jnp.bfloat16):
    level = level_of(stream_key, shape, cuts, -0.22, 0.18) if cuts else 1.0
    values = jax.random.normal(stream_key, shape, jnp.float32) * scale * level
    return jnp.minimum(jnp.maximum(values, -reach), reach).astype(dtype)


def setup_inputs(seed: int = 0) -> dict:
    key_of = jax.random.split(jax.random.key(seed), 6)
    return {
        "hidden": draw_hidden(jax.random.fold_in(key_of[5], 71), 0),
        "w_qkv": bell_draw(key_of[1], (D, COLS), D ** -0.5, 0.09375, ((0, 128),)),
        "bias_qkv": bell_draw(key_of[2], (COLS,), 0.5, 3.0),
        "doc_lengths": jax.vmap(lambda own: uneven(own, NDOC, SEQ, MAXDOC, 2))(jax.random.split(key_of[3], N_DP)).reshape((N_DP, NDOC)).astype(jnp.int32),
        "span_order": jax.vmap(lambda own: jax.random.permutation(own, N_CTX))(jax.random.split(key_of[4], N_DP)).reshape((N_DP, N_CTX)).astype(jnp.int32),
    }


NEG_FILL = -1e+30
ROPE_BASE = 1000000.0

def rope_tables(offsets):
    half_dim = HEAD_DIM // 2
    inverse = ROPE_BASE ** (-(jnp.arange(half_dim).astype(jnp.float32) * 2.0) / HEAD_DIM)
    angles = offsets.astype(jnp.float32)[:, None] * inverse[None, :]
    cosine = jnp.concatenate([jnp.cos(angles), jnp.cos(angles)], axis=1)
    sine = jnp.concatenate([jnp.sin(angles), jnp.sin(angles)], axis=1)
    return (cosine, sine)

def rotate(heads_in, cosine, sine):
    half_dim = heads_in.shape[-1] // 2
    turned = jnp.concatenate([-heads_in[..., half_dim:], heads_in[..., :half_dim]], axis=-1)
    return heads_in * cosine[:, None, :] + turned * sine[:, None, :]

def doc_starts(lengths_row, positions):
    ends = jnp.cumsum(lengths_row)
    starts = ends - lengths_row
    chosen = jnp.where(starts[None, :] <= positions[:, None], starts[None, :], 0)
    return lax.optimization_barrier(jnp.max(chosen, axis=1)).astype(jnp.int32)

def group_attention(rows, lengths_row, w_qkv, bias_qkv):
    positions = jnp.arange(SEQ).astype(jnp.int32)
    starts = doc_starts(lengths_row, positions)
    mixed = jnp.dot(rows, w_qkv, preferred_element_type=jnp.float32) + bias_qkv.astype(jnp.float32)
    query_cols = HEADS_Q * HEAD_DIM
    kv_cols = KV_HEADS * HEAD_DIM
    cosine, sine = rope_tables(positions - starts)
    queries = rotate(mixed[:, :query_cols].reshape(SEQ, HEADS_Q, HEAD_DIM), cosine, sine).astype(jnp.bfloat16)
    keys_rot = rotate(mixed[:, query_cols:query_cols + kv_cols].reshape(SEQ, KV_HEADS, HEAD_DIM), cosine, sine).astype(jnp.bfloat16)
    values = mixed[:, query_cols + kv_cols:].reshape(SEQ, KV_HEADS, HEAD_DIM).astype(jnp.bfloat16)
    block_rows = min(512, SEQ)
    blocks = SEQ // block_rows
    per_group = HEADS_Q // KV_HEADS
    keys_wide = keys_rot.astype(jnp.float32)
    values_wide = values.astype(jnp.float32)

    def one_block(inputs):
        query_block, query_pos, query_start = inputs
        grouped = query_block.reshape(block_rows, KV_HEADS, per_group, HEAD_DIM).astype(jnp.float32)
        scores = jnp.einsum('qgjd,kgd->gjqk', grouped, keys_wide, precision=lax.Precision.HIGHEST) * (1.0 / math.sqrt(HEAD_DIM))
        visible = (positions[None, :] >= query_start[:, None]) & (positions[None, :] <= query_pos[:, None])
        scores = jnp.where(visible[None, None], scores, NEG_FILL)
        highest = lax.optimization_barrier(jnp.max(scores, axis=-1, keepdims=True))
        weights = jnp.where(visible[None, None], jnp.exp(scores - highest), 0.0)
        totals = lax.optimization_barrier(jnp.sum(weights, axis=-1))
        rounded = lax.optimization_barrier(weights.astype(jnp.bfloat16))
        summed = jnp.einsum('gjqk,kgd->gjqd', rounded.astype(jnp.float32), values_wide, precision=lax.Precision.HIGHEST)
        result = summed / totals[..., None]
        return result.transpose(2, 0, 1, 3).reshape(block_rows, HEADS_Q * HEAD_DIM).astype(jnp.bfloat16)
    outputs = lax.map(one_block, (queries.reshape(blocks, block_rows, HEADS_Q, HEAD_DIM), positions.reshape(blocks, block_rows), starts.reshape(blocks, block_rows)))
    return outputs.reshape(SEQ, HEADS_Q * HEAD_DIM)

def reference(hidden, w_qkv, bias_qkv, doc_lengths, span_order):

    def per_group(inputs):
        rows, lengths_row, order_row = inputs
        row_index = jnp.arange(SEQ).astype(jnp.int32)
        row_pos = (order_row[row_index // TOK_DEV] * TOK_DEV + row_index % TOK_DEV).astype(jnp.int32)
        ordered = jnp.zeros_like(rows).at[row_pos].set(rows)
        result = group_attention(ordered, lengths_row, w_qkv, bias_qkv)
        return result[row_pos]
    return lax.map(per_group, (hidden, doc_lengths, span_order))
```

```python
import functools
import itertools
import math

import jax
import jax.numpy as jnp
import numpy as np
from jax import lax
from jax.experimental import pallas as pl
from jax.experimental.pallas import tpu as pltpu
from jax.sharding import Mesh, PartitionSpec as P

HEADS_Q = 14
KV_HEADS = 2
HEAD_DIM = 128
PER_KV = HEADS_Q // KV_HEADS
BLOCK = 512
BLOCKS = 8
RING = 4
CORE_ROWS = 28
SLOT = RING * CORE_ROWS
GROUP = 2 * RING * SLOT
TILE_Q = 256
TILE_K = 512
TILES = BLOCK // TILE_Q
TABLE_BLOCK = BLOCKS
TABLE_LOW = TABLE_BLOCK + 2 * TILES
TABLE_HIGH = TABLE_LOW + 2 * TILES
TABLE_RANGE = TABLE_HIGH + 2 * TILES
ROPE_BASE = 1000000.0
LOW = -1e30
MASKED = -2e38
EXP_SCALE = math.log2(math.e) / math.sqrt(HEAD_DIM)
MIB = 1 << 20
VMEM = 56 * MIB


def shift(block, axis, distance):
    return lax.ppermute(block, axis, [(i, (i + distance) % RING) for i in range(RING)])


def swap_cores(block):
    return lax.ppermute(block, "core", [(0, 1), (1, 0)])


def shift_by_core(block, axes, distance):
    route = []
    for y, z, x, core in itertools.product(range(RING), range(RING), range(RING), range(2)):
        at = {"y": y, "z": z}
        to = dict(at)
        to[axes[core]] = (at[axes[core]] + distance) % RING
        source = ((y * RING + z) * RING + x) * 2 + core
        route.append((source, ((to["y"] * RING + to["z"]) * RING + x) * 2 + core))
    return lax.ppermute(block, ("y", "z", "x", "core"), route)


def around(block, move):
    return [block, move(block, 1), move(block, 2), move(block, -1)]


EARLY, LATE = ("z", "y"), ("y", "z")


def gather_direct(block):
    n = block.shape[1] // 2
    mine = around(block, lambda a, d: shift_by_core(a, LATE, d))
    theirs = swap_cores(jnp.concatenate([piece[:, n:] for piece in mine], axis=0))
    return mine, [theirs]


def gather_onward(block):
    n = block.shape[1] // 2
    first = shift_by_core(block, LATE, 1)
    third = shift_by_core(block, LATE, -1)
    second_mine = shift_by_core(first[:, :n], LATE, 1)
    third_other = third[:, n:]
    second_other = shift_by_core(third_other, LATE, -1)
    theirs = swap_cores(jnp.concatenate([block[:, n:], first[:, n:], third_other], axis=0))
    far = swap_cores(second_other)
    return [block, first, second_mine, third], [theirs, far]


def arrange_kernel(heads_of, place_ref, weight_ref, out_ref):
    first = place_ref[3] == 0
    for at, (zero, one) in enumerate(zip(*heads_of)):
        out_ref[:, at * HEAD_DIM : (at + 1) * HEAD_DIM] = jnp.where(
            first,
            weight_ref[:, zero * HEAD_DIM : (zero + 1) * HEAD_DIM],
            weight_ref[:, one * HEAD_DIM : (one + 1) * HEAD_DIM],
        )


def arrange(place, array, heads_of):
    spec = pl.BlockSpec(array.shape, lambda i, place: (0, 0))
    return pl.pallas_call(
        functools.partial(arrange_kernel, heads_of),
        grid_spec=pltpu.PrefetchScalarGridSpec(num_scalar_prefetch=1, grid=(1,), in_specs=[spec], out_specs=spec),
        out_shape=jax.ShapeDtypeStruct(array.shape, array.dtype),
        compiler_params=pltpu.CompilerParams(vmem_limit_bytes=VMEM),
    )(place, array)


def stack_kernel(cut, *refs):
    parts, outs = refs[:RING], refs[RING:]
    rows = jnp.concatenate([part[...] for part in parts], axis=0)
    outs[0][...] = rows[:, :cut]
    outs[1][...] = rows[:, cut:]


def stack(parts, cut):
    rows, width = RING * parts[0].shape[0], parts[0].shape[1]
    vmem = pl.BlockSpec(memory_space=pltpu.VMEM)
    return pl.pallas_call(
        functools.partial(stack_kernel, cut),
        in_specs=[vmem] * RING,
        out_specs=[vmem] * 2,
        out_shape=[
            jax.ShapeDtypeStruct((rows, cut), parts[0].dtype),
            jax.ShapeDtypeStruct((rows, width - cut), parts[0].dtype),
        ],
        compiler_params=pltpu.CompilerParams(vmem_limit_bytes=VMEM),
    )(*parts)


def permute_kernel(source_ref, rows_ref, out_ref, matrix):
    @pl.when(pl.program_id(0) == 0)
    def _():
        row = lax.broadcasted_iota(jnp.int32, matrix.shape, 0)
        matrix[...] = jnp.where(row == source_ref[...], 1.0, 0.0).astype(jnp.bfloat16)

    out_ref[...] = jnp.dot(
        rows_ref[...], matrix[...], preferred_element_type=jnp.float32
    ).astype(jnp.bfloat16)


def permute_columns(source, rows):
    width = source.shape[1]
    count = rows.shape[1] // width
    by_group = pl.BlockSpec((rows.shape[0], width), lambda i: (0, i))
    return pl.pallas_call(
        permute_kernel,
        grid=(count,),
        in_specs=[pl.BlockSpec((1, width), lambda i: (0, 0)), by_group],
        out_specs=by_group,
        scratch_shapes=[pltpu.VMEM((width, width), jnp.bfloat16)],
        out_shape=jax.ShapeDtypeStruct(rows.shape, jnp.bfloat16),
        compiler_params=pltpu.CompilerParams(vmem_limit_bytes=VMEM),
        cost_estimate=pl.CostEstimate(
            flops=2 * rows.shape[0] * rows.shape[1] * width,
            bytes_accessed=4 * rows.shape[0] * rows.shape[1],
            transcendentals=0,
        ),
    )(source, rows)


def project_kernel(columns, counts, rotated, place_ref, own_ref, partner_ref, bias_ref, cos_ref, sin_ref, *refs):
    mine, theirs = refs[: counts[0]], refs[counts[0] : sum(counts)]
    out_ref, weight, total, sems = refs[sum(counts) :]
    step = pl.program_id(0)
    z, core = place_ref[1], place_ref[3]

    def copy_of(family, behind, slot):
        part = core if family == 0 else 1 - core
        behind_y = jnp.where(part == 0, behind, slot)
        behind_z = jnp.where(part == 0, slot, behind)
        row = behind_y * GROUP + part * (GROUP // 2) + lax.rem(z + RING - behind_z, RING) * SLOT
        if family == 0:
            ref, first = mine[behind], slot * SLOT
        elif len(theirs) == 1:
            ref, first = theirs[0], (behind * RING + slot) * SLOT
        elif behind == 2:
            ref, first = theirs[1], slot * SLOT
        else:
            ref, first = theirs[0], (min(behind, 2) * RING + slot) * SLOT
        return pltpu.make_async_copy(
            ref.at[pl.ds(first, SLOT), pl.ds(0, columns)],
            weight.at[pl.ds(pl.multiple_of(row, 16), SLOT), :],
            sems.at[behind_y, family * RING + jnp.where(part == 0, slot, behind)],
        )

    @pl.when(step == 0)
    def _():
        for family in range(2):
            for behind in range(RING):
                for slot in range(RING):
                    copy_of(family, behind, slot).start()
        total[...] = jnp.broadcast_to(bias_ref[...], total.shape)

    for i in range(2 * RING):
        pltpu.make_async_copy(
            mine[0].at[pl.ds(0, SLOT), pl.ds(0, columns)], weight.at[pl.ds(0, SLOT), :], sems.at[step, i]
        ).wait()
    group = weight[pl.ds(pl.multiple_of(step * GROUP, GROUP), GROUP), :]
    for half, rows_ref in enumerate((own_ref, partner_ref)):
        total[half * BLOCK : (half + 1) * BLOCK] += jnp.dot(
            rows_ref[...], group, preferred_element_type=jnp.float32
        )

    @pl.when(step == RING - 1)
    def _():
        for head in range(columns // HEAD_DIM):
            lanes = slice(head * HEAD_DIM, (head + 1) * HEAD_DIM)
            one = total[:, lanes]
            if head < rotated:
                one = one * cos_ref[...] + pltpu.roll(one, HEAD_DIM // 2, 1) * sin_ref[...]
            out_ref[:, lanes] = one.astype(jnp.bfloat16)


def project(place, own, partner, bias, cosine, sine, pieces, rotated):
    mine, theirs = pieces
    columns = bias.shape[1]
    depth = own.shape[1]
    any_spec = pl.BlockSpec(memory_space=pl.ANY)
    rows = pl.BlockSpec((BLOCK, GROUP), lambda i, place: (0, lax.rem(place[0] + RING - i, RING)))
    whole = pl.BlockSpec((2 * BLOCK, HEAD_DIM), lambda i, place: (0, 0))
    return pl.pallas_call(
        functools.partial(project_kernel, columns, (len(mine), len(theirs)), rotated),
        grid_spec=pltpu.PrefetchScalarGridSpec(
            num_scalar_prefetch=1,
            grid=(RING,),
            in_specs=[rows, rows, pl.BlockSpec((1, columns), lambda i, place: (0, 0)), whole, whole]
            + [any_spec] * (len(mine) + len(theirs)),
            out_specs=pl.BlockSpec((2 * BLOCK, columns), lambda i, place: (0, 0)),
            scratch_shapes=[
                pltpu.VMEM((depth, columns), jnp.bfloat16),
                pltpu.VMEM((2 * BLOCK, columns), jnp.float32),
                pltpu.SemaphoreType.DMA((RING, 2 * RING)),
            ],
        ),
        out_shape=jax.ShapeDtypeStruct((2 * BLOCK, columns), jnp.bfloat16),
        compiler_params=pltpu.CompilerParams(vmem_limit_bytes=VMEM),
        cost_estimate=pl.CostEstimate(
            flops=4 * BLOCK * depth * columns,
            bytes_accessed=4 * BLOCK * depth + 2 * depth * columns,
            transcendentals=0,
        ),
    )(place, own, partner, bias, cosine, sine, *mine, *theirs)


def attend_kernel(heads, table_ref, query_ref, start_ref, *refs):
    pieces = refs[:RING]
    their_ref, my_ref, kept, stacked, maxima, totals, summed, sems = refs[RING:]
    step = pl.program_id(0)
    block = table_ref[TABLE_BLOCK + step]
    low = table_ref[TABLE_LOW + step]
    high = table_ref[TABLE_HIGH + step]

    def each_block(act):
        def one(b, carry):
            slot = table_ref[b]
            for s in range(BLOCKS):

                @pl.when(slot == s)
                def _():
                    act(
                        pltpu.make_async_copy(
                            pieces[s // 2].at[pl.ds((s % 2) * BLOCK, BLOCK), :], kept.at[b], sems.at[b]
                        )
                    )

            return carry

        lax.fori_loop(table_ref[TABLE_RANGE], table_ref[TABLE_RANGE + 1], one, 0)

    @pl.when(step == 0)
    def _():
        each_block(lambda copy: copy.start())

    row_first = block * BLOCK + lax.rem(step, TILES) * TILE_Q
    tile_low = low // TILE_K
    tile_end = (row_first + TILE_Q + TILE_K - 1) // TILE_K
    rows = heads * TILE_Q
    maxima[...] = jnp.full(maxima.shape, LOW, jnp.float32)
    totals[...] = jnp.zeros(totals.shape, jnp.float32)
    summed[...] = jnp.zeros(summed.shape, jnp.float32)
    for head in range(heads):
        stacked[head * TILE_Q : (head + 1) * TILE_Q] = query_ref[:, head * HEAD_DIM : (head + 1) * HEAD_DIM]
    starts = start_ref[...]
    row_pos = row_first + lax.broadcasted_iota(jnp.int32, (TILE_Q, TILE_K), 0)
    per_block = BLOCK // TILE_K

    @pl.when(step == 0)
    def _():
        each_block(lambda copy: copy.wait())

    def at_tile(t, column):
        lanes_of = pl.ds(column * HEAD_DIM, HEAD_DIM)
        if per_block == 1:
            return kept[t, :, lanes_of]
        return kept[t // per_block, pl.ds(pl.multiple_of(lax.rem(t, per_block) * TILE_K, TILE_K), TILE_K), lanes_of]

    def lanes(values_in):
        return [values_in[:, i * HEAD_DIM : (i + 1) * HEAD_DIM] for i in range(values_in.shape[1] // HEAD_DIM)]

    def visit(t, masked):
        found = lax.dot_general(
            stacked[...], at_tile(t, 0), (((1,), (1,)), ((), ())), preferred_element_type=jnp.float32
        )
        if masked:
            key_pos = t * TILE_K + lax.broadcasted_iota(jnp.int32, (TILE_Q, TILE_K), 1)
            visible = (key_pos >= starts) & (key_pos <= row_pos)
            found = jnp.where(visible[None], found.reshape(heads, TILE_Q, TILE_K), MASKED).reshape(rows, TILE_K)
        before = maxima[...]
        top = functools.reduce(jnp.maximum, lanes(found))
        top = jnp.maximum(before, jnp.max(top, axis=1, keepdims=True))
        factor = jnp.exp2((before - top) * EXP_SCALE)
        weights = [jnp.exp2((part - top) * EXP_SCALE) for part in lanes(found)]
        maxima[...] = top
        totals[...] = totals[...] * factor + functools.reduce(jnp.add, weights)
        rounded = jnp.concatenate([w.astype(jnp.bfloat16) for w in weights], axis=1)
        summed[...] = summed[...] * factor + jnp.dot(rounded, at_tile(t, 1), preferred_element_type=jnp.float32)

    def one_tile(t, carry):
        whole = (t * TILE_K >= high) & ((t + 1) * TILE_K <= row_first + 1)

        @pl.when(whole)
        def _():
            visit(t, False)

        @pl.when(jnp.logical_not(whole))
        def _():
            visit(t, True)

        return carry

    lax.fori_loop(tile_low, tile_end, one_tile, 0)
    result = summed[...] / jnp.sum(totals[...], axis=1, keepdims=True)

    def store(out_ref):
        for head in range(heads):
            out_ref[:, head * HEAD_DIM : (head + 1) * HEAD_DIM] = result[
                head * TILE_Q : (head + 1) * TILE_Q
            ].astype(jnp.bfloat16)

    @pl.when(step < TILES)
    def _():
        store(their_ref)

    @pl.when(step >= TILES)
    def _():
        store(my_ref)


def attend(table, queries, starts, pieces):
    heads = queries.shape[1] // HEAD_DIM

    def rows_of(width):
        return pl.BlockSpec((TILE_Q, width), lambda i, table: (lax.rem(i + TILES, 2 * TILES), 0))

    wide = (TILE_Q, heads * HEAD_DIM)
    return pl.pallas_call(
        functools.partial(attend_kernel, heads),
        grid_spec=pltpu.PrefetchScalarGridSpec(
            num_scalar_prefetch=1,
            grid=(2 * TILES,),
            in_specs=[rows_of(heads * HEAD_DIM), rows_of(1)] + [pl.BlockSpec(memory_space=pl.ANY)] * RING,
            out_specs=[
                pl.BlockSpec(wide, lambda i, table: (jnp.minimum(i, TILES - 1), 0)),
                pl.BlockSpec(wide, lambda i, table: (jnp.maximum(i - TILES, 0), 0)),
            ],
            scratch_shapes=[
                pltpu.VMEM((BLOCKS, BLOCK, 2 * HEAD_DIM), jnp.bfloat16),
                pltpu.VMEM((heads * TILE_Q, HEAD_DIM), jnp.bfloat16),
                pltpu.VMEM((heads * TILE_Q, HEAD_DIM), jnp.float32),
                pltpu.VMEM((heads * TILE_Q, HEAD_DIM), jnp.float32),
                pltpu.VMEM((heads * TILE_Q, HEAD_DIM), jnp.float32),
                pltpu.SemaphoreType.DMA((BLOCKS,)),
            ],
        ),
        out_shape=[jax.ShapeDtypeStruct((BLOCK, heads * HEAD_DIM), jnp.bfloat16)] * 2,
        compiler_params=pltpu.CompilerParams(vmem_limit_bytes=VMEM),
        cost_estimate=pl.CostEstimate(
            flops=heads * 2 * BLOCK * 1024 * HEAD_DIM * 4,
            bytes_accessed=4 * MIB,
            transcendentals=heads * 2 * BLOCK * 1024,
        ),
    )(table, queries, starts, *pieces)


def body(hidden, w_qkv, bias_qkv, doc_lengths, span_order):
    x, core = lax.axis_index("x"), lax.axis_index("core")
    place = jnp.stack([lax.axis_index("y"), lax.axis_index("z"), x, core]).astype(jnp.int32)

    heads = [[HEADS_Q + g, HEADS_Q + KV_HEADS + g] + [g * PER_KV + i for i in range(PER_KV)] for g in range(KV_HEADS)]
    cuts = (0, 2, 6, 9)
    heads_of = [
        [h for a, b in zip(cuts, cuts[1:]) for side in (g, 1 - g) for h in heads[side][a:b]] for g in range(2)
    ]
    chunk = arrange(place, w_qkv, heads_of)
    kv = 2 * HEAD_DIM
    kv_slot, q_slot = stack(around(chunk, lambda a, d: shift(a, "x", d)), 2 * kv)

    def early(part):
        return around(part, lambda a, d: shift_by_core(a, EARLY, d))

    kv_early = early(kv_slot)
    kv_block = jnp.concatenate(kv_early, axis=0)
    kv_block, q_slot, hidden = lax.optimization_barrier((kv_block, q_slot, hidden))
    kv_pieces = gather_direct(kv_block)
    q_early = early(q_slot)
    width = 8 * HEAD_DIM
    one_block = jnp.concatenate([p[:, :width] for p in q_early], axis=0)
    two_block = jnp.concatenate([p[:, width:] for p in q_early], axis=0)
    one_pieces = gather_onward(one_block)
    two_pieces = gather_onward(two_block)

    group = jnp.arange(GROUP, dtype=jnp.int32)
    in_slot = group % SLOT
    source = (
        (group % (GROUP // 2)) // SLOT * (2 * SLOT)
        + (x + RING - in_slot // CORE_ROWS) % RING * (2 * CORE_ROWS)
        + group // (GROUP // 2) * CORE_ROWS
        + in_slot % CORE_ROWS
    )
    own = permute_columns(source[None].astype(jnp.int32), hidden[0])
    partner = swap_cores(own)

    bias_heads = bias_qkv.astype(jnp.float32).reshape(-1, HEAD_DIM)
    bias = jnp.where(
        core == 0, bias_heads[np.array(heads[0])].reshape(1, -1), bias_heads[np.array(heads[1])].reshape(1, -1)
    )

    order = span_order[0]
    lengths = doc_lengths[0]
    count = lengths.shape[0]
    before = jnp.arange(count)[:, None] > jnp.arange(count)[None, :]
    begins = jnp.sum(jnp.where(before, lengths[None, :], 0), axis=1)
    first_block = order[2 * x + core]
    second_block = order[2 * x + 1 - core]
    inside = jnp.arange(BLOCK, dtype=jnp.int32)
    positions = jnp.concatenate([first_block * BLOCK + inside, second_block * BLOCK + inside])
    starts = jnp.max(jnp.where(begins[None, :] <= positions[:, None], begins[None, :], 0), axis=1)
    half = HEAD_DIM // 2
    inverse = ROPE_BASE ** (-(jnp.arange(half).astype(jnp.float32) * 2.0) / HEAD_DIM)
    angles = (positions - starts).astype(jnp.float32)[:, None] * inverse[None, :]
    cosine, sine = jnp.cos(angles), jnp.sin(angles)
    cosine = jnp.concatenate([cosine, cosine], axis=1)
    sine = jnp.concatenate([-sine, sine], axis=1)

    slots = jnp.arange(BLOCKS, dtype=jnp.int32)
    holder = 2 * ((x + RING - slots // 2) % RING) + (core + slots % 2) % 2
    block_of_slot = jnp.sum(jnp.where(holder[:, None] == jnp.arange(BLOCKS)[None, :], order[None, :], 0), axis=1)
    slot_of_block = jnp.sum(
        jnp.where(block_of_slot[None, :] == jnp.arange(BLOCKS)[:, None], slots[None, :], 0), axis=1
    )
    by_tile = jnp.roll(starts.reshape(2 * TILES, TILE_Q), TILES, axis=0)
    block_of_step = jnp.stack([second_block] * TILES + [first_block] * TILES)
    lows, highs = by_tile[:, 0], by_tile[:, -1]
    span = jnp.stack([jnp.min(lows) // BLOCK, jnp.maximum(first_block, second_block) + 1])
    table = jnp.concatenate([slot_of_block, block_of_step, lows, highs, span]).astype(jnp.int32)
    start_column = starts[:, None].astype(jnp.int32)

    pairs = project(place, own, partner, bias[:, :kv], cosine, sine, kv_pieces, 1)
    all_pairs = around(pairs, lambda a, d: shift(a, "x", d))
    one = project(place, own, partner, bias[:, kv : 3 * kv], cosine, sine, one_pieces, 4)
    two = project(place, own, partner, bias[:, 3 * kv :], cosine, sine, two_pieces, 3)
    theirs, mine = [], []
    for queries in (one, two):
        their_rows, my_rows = attend(table, queries, start_column, all_pairs)
        theirs.append(swap_cores(their_rows))
        mine.append(my_rows)
    result = jnp.where(
        core == 0, jnp.concatenate(mine + theirs, axis=1), jnp.concatenate(theirs + mine, axis=1)
    )
    return result[None]


def solution(mesh):
    fine = Mesh(mesh.devices.reshape(RING, RING, RING, 2), ("y", "z", "x", "core"))
    rows = P(("y", "z"), ("x", "core"), None)
    in_specs = (rows, P(("y", "z", "x", "core"), None), P(), P(("y", "z"), None), P(("y", "z"), None))
    return jax.shard_map(body, mesh=fine, in_specs=in_specs, out_specs=rows, check_vma=False)
```

```python
import functools
import itertools
import math

import jax
import jax.numpy as jnp
import numpy as np
from jax import lax
from jax.experimental import pallas as pl
from jax.experimental.pallas import tpu as pltpu
from jax.sharding import Mesh, PartitionSpec as P

HEADS_Q = 14
KV_HEADS = 2
HEAD_DIM = 128
PER_KV = HEADS_Q // KV_HEADS
BLOCK = 512
BLOCKS = 8
RING = 4
CORE_ROWS = 28
SLOT = RING * CORE_ROWS
GROUP = 2 * RING * SLOT
TILE_Q = 512
TILE_K = 512
TILES = BLOCK // TILE_Q
TABLE_BLOCK = BLOCKS
TABLE_LOW = TABLE_BLOCK + 2 * TILES
TABLE_HIGH = TABLE_LOW + 2 * TILES
TABLE_RANGE = TABLE_HIGH + 2 * TILES
TABLE_CORE = TABLE_RANGE + 2
ROPE_BASE = 1000000.0
LOW = -1e30
MASKED = -2e38
EXP_SCALE = math.log2(math.e) / math.sqrt(HEAD_DIM)
MIB = 1 << 20
VMEM = 24 * MIB
VMEM_ATTEND = 40 * MIB


def shift(block, axis, distance):
    return lax.ppermute(block, axis, [(i, (i + distance) % RING) for i in range(RING)])


def swap_cores(block):
    return lax.ppermute(block, "core", [(0, 1), (1, 0)])


def shift_by_core(block, axes, distance):
    route = []
    for y, z, x, core in itertools.product(range(RING), range(RING), range(RING), range(2)):
        at = {"y": y, "z": z}
        to = dict(at)
        to[axes[core]] = (at[axes[core]] + distance) % RING
        source = ((y * RING + z) * RING + x) * 2 + core
        route.append((source, ((to["y"] * RING + to["z"]) * RING + x) * 2 + core))
    return lax.ppermute(block, ("y", "z", "x", "core"), route)


def around(block, move):
    return [block, move(block, 1), move(block, 2), move(block, -1)]


EARLY, LATE = ("z", "y"), ("y", "z")


def after(value, *others):
    return lax.optimization_barrier((value, *others))[0]


def gather_direct(block):
    mine = around(block, lambda a, d: shift_by_core(a, LATE, d))
    return mine, [swap_cores(piece) for piece in mine]


def gather_near(block):
    return shift_by_core(block, LATE, 1), shift_by_core(block, LATE, -1)


def gather_far(block, first, third, before):
    n = block.shape[1] // 2
    second_mine = shift_by_core(first[:, :n], LATE, 1)
    third_other = third[:, n:]
    second_other = shift_by_core(third_other, LATE, -1)
    near_other = jnp.concatenate([block[:, n:], first[:, n:], third_other], axis=0)
    near_other, second_other, second_mine = lax.optimization_barrier(
        (near_other, second_other, second_mine, *before)
    )[:3]
    theirs, far = swap_cores(near_other), swap_cores(second_other)
    return [block, first, second_mine, third], [theirs, far]


def arrange_kernel(heads_of, place_ref, weight_ref, out_ref):
    first = place_ref[3] == 0
    for at, (zero, one) in enumerate(zip(*heads_of)):
        out_ref[:, at * HEAD_DIM : (at + 1) * HEAD_DIM] = jnp.where(
            first,
            weight_ref[:, zero * HEAD_DIM : (zero + 1) * HEAD_DIM],
            weight_ref[:, one * HEAD_DIM : (one + 1) * HEAD_DIM],
        )


def arrange(place, array, heads_of):
    spec = pl.BlockSpec(array.shape, lambda i, place: (0, 0))
    return pl.pallas_call(
        functools.partial(arrange_kernel, heads_of),
        grid_spec=pltpu.PrefetchScalarGridSpec(num_scalar_prefetch=1, grid=(1,), in_specs=[spec], out_specs=spec),
        out_shape=jax.ShapeDtypeStruct(array.shape, array.dtype),
        compiler_params=pltpu.CompilerParams(vmem_limit_bytes=VMEM),
    )(place, array)


def stack_kernel(*refs):
    parts, out = refs[:RING], refs[RING]
    out[...] = jnp.concatenate([part[...] for part in parts], axis=0)


def stack(parts):
    rows, width = parts[0].shape
    whole = pl.BlockSpec((rows, width), lambda i: (0, 0))
    return pl.pallas_call(
        stack_kernel,
        grid=(1,),
        in_specs=[whole] * RING,
        out_specs=pl.BlockSpec((RING * rows, width), lambda i: (0, 0)),
        out_shape=jax.ShapeDtypeStruct((RING * rows, width), parts[0].dtype),
        compiler_params=pltpu.CompilerParams(vmem_limit_bytes=VMEM),
    )(*parts)


def place_kernel(cuts, *refs):
    parts, outs, sems = refs[:RING], refs[RING:-1], refs[-1]
    rows = parts[0].shape[0]
    copies = [
        pltpu.make_async_copy(
            part.at[:, pl.ds(a, b - a)], out.at[pl.ds(i * rows, rows), :], sems.at[n, i]
        )
        for n, (out, a, b) in enumerate(zip(outs, cuts, cuts[1:]))
        for i, part in enumerate(parts)
    ]
    for copy in copies:
        copy.start()
    for copy in copies:
        copy.wait()


def place_rows(parts, cuts):
    rows = RING * parts[0].shape[0]
    shapes = [(rows, b - a) for a, b in zip(cuts, cuts[1:])]
    return pl.pallas_call(
        functools.partial(place_kernel, cuts),
        grid=(1,),
        in_specs=[pl.BlockSpec(memory_space=pl.ANY)] * RING,
        out_specs=[pl.BlockSpec(shape, lambda i: (0, 0)) for shape in shapes],
        out_shape=[jax.ShapeDtypeStruct(shape, parts[0].dtype) for shape in shapes],
        scratch_shapes=[pltpu.SemaphoreType.DMA((len(shapes), RING))],
        compiler_params=pltpu.CompilerParams(vmem_limit_bytes=VMEM),
    )(*parts)


def permute_kernel(source_ref, rows_ref, out_ref, matrix):
    @pl.when(pl.program_id(0) == 0)
    def _():
        row = lax.broadcasted_iota(jnp.int32, matrix.shape, 0)
        matrix[...] = jnp.where(row == source_ref[...], 1.0, 0.0).astype(jnp.bfloat16)

    out_ref[...] = jnp.dot(
        rows_ref[...], matrix[...], preferred_element_type=jnp.float32
    ).astype(jnp.bfloat16)


def permute_columns(source, rows):
    width = source.shape[1]
    count = rows.shape[1] // width
    by_group = pl.BlockSpec((rows.shape[0], width), lambda i: (0, i))
    return pl.pallas_call(
        permute_kernel,
        grid=(count,),
        in_specs=[pl.BlockSpec((1, width), lambda i: (0, 0)), by_group],
        out_specs=by_group,
        scratch_shapes=[pltpu.VMEM((width, width), jnp.bfloat16)],
        out_shape=jax.ShapeDtypeStruct(rows.shape, jnp.bfloat16),
        compiler_params=pltpu.CompilerParams(vmem_limit_bytes=VMEM),
    )(source, rows)


def project_kernel(columns, counts, rotated, place_ref, own_ref, partner_ref, bias_ref, cos_ref, sin_ref, *refs):
    mine, theirs = refs[: counts[0]], refs[counts[0] : sum(counts)]
    out_ref, weight, total, sems = refs[sum(counts) :]
    step = pl.program_id(0)
    z, core = place_ref[1], place_ref[3]

    def copy_of(family, behind, slot):
        part = core if family == 0 else 1 - core
        behind_y = jnp.where(part == 0, behind, slot)
        behind_z = jnp.where(part == 0, slot, behind)
        row = behind_y * GROUP + part * (GROUP // 2) + lax.rem(z + RING - behind_z, RING) * SLOT
        column = 0
        if family == 0:
            ref, first = mine[behind], slot * SLOT
        elif len(theirs) == RING:
            ref, first, column = theirs[behind], slot * SLOT, columns
        elif behind == 2:
            ref, first = theirs[1], slot * SLOT
        else:
            ref, first = theirs[0], (min(behind, 2) * RING + slot) * SLOT
        return pltpu.make_async_copy(
            ref.at[pl.ds(first, SLOT), pl.ds(column, columns)],
            weight.at[pl.ds(pl.multiple_of(row, 16), SLOT), :],
            sems.at[behind_y, family * RING + jnp.where(part == 0, slot, behind)],
        )

    def start_group(behind_y):
        for first_part in range(2):

            @pl.when(core == first_part)
            def _():
                for family in range(2):
                    for other in range(RING):
                        if (family + first_part) % 2 == 0:
                            copy_of(family, behind_y, other).start()
                        else:
                            copy_of(family, other, behind_y).start()

    for group in range(RING):

        @pl.when(step == max(group - 1, 0))
        def _():
            start_group(group)

    @pl.when(step == 0)
    def _():
        total[...] = jnp.broadcast_to(bias_ref[...], total.shape)

    for i in range(2 * RING):
        pltpu.make_async_copy(
            mine[0].at[pl.ds(0, SLOT), pl.ds(0, columns)], weight.at[pl.ds(0, SLOT), :], sems.at[step, i]
        ).wait()
    group = weight[pl.ds(pl.multiple_of(step * GROUP, GROUP), GROUP), :]
    for half, rows_ref in enumerate((own_ref, partner_ref)):
        total[half * BLOCK : (half + 1) * BLOCK] += jnp.dot(
            rows_ref[...], group, preferred_element_type=jnp.float32
        )

    @pl.when(step == RING - 1)
    def _():
        for head in range(columns // HEAD_DIM):
            lanes = slice(head * HEAD_DIM, (head + 1) * HEAD_DIM)
            one = total[:, lanes]
            if head < rotated:
                one = one * cos_ref[...] + pltpu.roll(one, HEAD_DIM // 2, 1) * sin_ref[...]
            out_ref[:, lanes] = one.astype(jnp.bfloat16)


def project(place, own, partner, bias, cosine, sine, pieces, rotated):
    mine, theirs = pieces
    columns = bias.shape[1]
    depth = own.shape[1]
    any_spec = pl.BlockSpec(memory_space=pl.ANY)
    rows = pl.BlockSpec((BLOCK, GROUP), lambda i, place: (0, lax.rem(place[0] + RING - i, RING)))
    whole = pl.BlockSpec((2 * BLOCK, HEAD_DIM), lambda i, place: (0, 0))
    return pl.pallas_call(
        functools.partial(project_kernel, columns, (len(mine), len(theirs)), rotated),
        grid_spec=pltpu.PrefetchScalarGridSpec(
            num_scalar_prefetch=1,
            grid=(RING,),
            in_specs=[rows, rows, pl.BlockSpec((1, columns), lambda i, place: (0, 0)), whole, whole]
            + [any_spec] * (len(mine) + len(theirs)),
            out_specs=pl.BlockSpec((2 * BLOCK, columns), lambda i, place: (0, 0)),
            scratch_shapes=[
                pltpu.VMEM((depth, columns), jnp.bfloat16),
                pltpu.VMEM((2 * BLOCK, columns), jnp.float32),
                pltpu.SemaphoreType.DMA((RING, 2 * RING)),
            ],
        ),
        out_shape=jax.ShapeDtypeStruct((2 * BLOCK, columns), jnp.bfloat16),
        compiler_params=pltpu.CompilerParams(vmem_limit_bytes=VMEM),
    )(place, own, partner, bias, cosine, sine, *mine, *theirs)


def attend_kernel(heads, table_ref, query_ref, start_ref, *refs):
    pieces = refs[: RING + 1]
    their_ref, my_ref, kept, stacked, maxima, totals, summed, sems = refs[RING + 1 :]
    step = pl.program_id(0)
    block = table_ref[TABLE_BLOCK + step]
    low = table_ref[TABLE_LOW + step]
    high = table_ref[TABLE_HIGH + step]

    def each_block(act):
        def one(b, carry):
            slot = table_ref[b]
            for s in range(BLOCKS):

                @pl.when(slot == s)
                def _():
                    rows = pl.ds((s % 2) * BLOCK, BLOCK)
                    if s // 2 == 2:
                        for n in range(2):
                            act(
                                pltpu.make_async_copy(
                                    pieces[2 + n].at[rows, :],
                                    kept.at[b, :, pl.ds(n * HEAD_DIM, HEAD_DIM)],
                                    sems.at[n, b],
                                )
                            )
                    else:
                        piece = pieces[s // 2 if s // 2 < 2 else RING]
                        act(pltpu.make_async_copy(piece.at[rows, :], kept.at[b], sems.at[0, b]))

            return carry

        lax.fori_loop(table_ref[TABLE_RANGE], table_ref[TABLE_RANGE + 1], one, 0)

    @pl.when(step == 0)
    def _():
        each_block(lambda copy: copy.start())

    row_first = block * BLOCK + lax.rem(step, TILES) * TILE_Q
    tile_low = low // TILE_K
    tile_end = (row_first + TILE_Q + TILE_K - 1) // TILE_K
    rows = heads * TILE_Q
    maxima[...] = jnp.full(maxima.shape, LOW, jnp.float32)
    totals[...] = jnp.zeros(totals.shape, jnp.float32)
    summed[...] = jnp.zeros(summed.shape, jnp.float32)
    for head in range(heads):
        stacked[head * TILE_Q : (head + 1) * TILE_Q] = query_ref[:, head * HEAD_DIM : (head + 1) * HEAD_DIM]
    starts = start_ref[...]
    row_pos = row_first + lax.broadcasted_iota(jnp.int32, (TILE_Q, TILE_K), 0)
    per_block = BLOCK // TILE_K

    @pl.when(step == 0)
    def _():
        each_block(lambda copy: copy.wait())

    def at_tile(t, column):
        lanes_of = pl.ds(column * HEAD_DIM, HEAD_DIM)
        if per_block == 1:
            return kept[t, :, lanes_of]
        return kept[t // per_block, pl.ds(pl.multiple_of(lax.rem(t, per_block) * TILE_K, TILE_K), TILE_K), lanes_of]

    def lanes(values_in):
        return [values_in[:, i * HEAD_DIM : (i + 1) * HEAD_DIM] for i in range(values_in.shape[1] // HEAD_DIM)]

    def visit(t, masked):
        found = lax.dot_general(
            stacked[...], at_tile(t, 0), (((1,), (1,)), ((), ())), preferred_element_type=jnp.float32
        )
        if masked:
            key_pos = t * TILE_K + lax.broadcasted_iota(jnp.int32, (TILE_Q, TILE_K), 1)
            visible = (key_pos >= starts) & (key_pos <= row_pos)
            found = jnp.where(visible[None], found.reshape(heads, TILE_Q, TILE_K), MASKED).reshape(rows, TILE_K)
        before = maxima[...]
        top = functools.reduce(jnp.maximum, lanes(found))
        top = jnp.maximum(before, jnp.max(top, axis=1, keepdims=True))
        factor = jnp.exp2((before - top) * EXP_SCALE)
        weights = [jnp.exp2((part - top) * EXP_SCALE) for part in lanes(found)]
        maxima[...] = top
        totals[...] = totals[...] * factor + functools.reduce(jnp.add, weights)
        rounded = jnp.concatenate([w.astype(jnp.bfloat16) for w in weights], axis=1)
        summed[...] = summed[...] * factor + jnp.dot(rounded, at_tile(t, 1), preferred_element_type=jnp.float32)

    def one_tile(t, carry):
        whole = (t * TILE_K >= high) & ((t + 1) * TILE_K <= row_first + 1)

        @pl.when(whole)
        def _():
            visit(t, False)

        @pl.when(jnp.logical_not(whole))
        def _():
            visit(t, True)

        return carry

    lax.fori_loop(tile_low, tile_end, one_tile, 0)
    result = summed[...] / jnp.sum(totals[...], axis=1, keepdims=True)

    def store(out_ref):
        for head in range(heads):
            out_ref[:, head * HEAD_DIM : (head + 1) * HEAD_DIM] = result[
                head * TILE_Q : (head + 1) * TILE_Q
            ].astype(jnp.bfloat16)

    @pl.when(step < TILES)
    def _():
        store(their_ref)

    @pl.when(step >= TILES)
    def _():
        store(my_ref)


def attend(table, queries, starts, pieces):
    heads = queries.shape[1] // HEAD_DIM

    def rows_of(width):
        return pl.BlockSpec((TILE_Q, width), lambda i, table: (lax.rem(i + TILES, 2 * TILES), 0))

    wide = (TILE_Q, heads * HEAD_DIM)
    return pl.pallas_call(
        functools.partial(attend_kernel, heads),
        grid_spec=pltpu.PrefetchScalarGridSpec(
            num_scalar_prefetch=1,
            grid=(2 * TILES,),
            in_specs=[rows_of(heads * HEAD_DIM), rows_of(1)] + [pl.BlockSpec(memory_space=pl.ANY)] * (RING + 1),
            out_specs=[
                pl.BlockSpec(wide, lambda i, table: (jnp.minimum(i, TILES - 1), 0)),
                pl.BlockSpec(wide, lambda i, table: (jnp.maximum(i - TILES, 0), table[TABLE_CORE])),
            ],
            scratch_shapes=[
                pltpu.VMEM((BLOCKS, BLOCK, 2 * HEAD_DIM), jnp.bfloat16),
                pltpu.VMEM((heads * TILE_Q, HEAD_DIM), jnp.bfloat16),
                pltpu.VMEM((heads * TILE_Q, HEAD_DIM), jnp.float32),
                pltpu.VMEM((heads * TILE_Q, HEAD_DIM), jnp.float32),
                pltpu.VMEM((heads * TILE_Q, HEAD_DIM), jnp.float32),
                pltpu.SemaphoreType.DMA((2, BLOCKS)),
            ],
        ),
        out_shape=[
            jax.ShapeDtypeStruct((BLOCK, heads * HEAD_DIM), jnp.bfloat16),
            jax.ShapeDtypeStruct((BLOCK, KV_HEADS * heads * HEAD_DIM), jnp.bfloat16),
        ],
        compiler_params=pltpu.CompilerParams(vmem_limit_bytes=VMEM_ATTEND),
    )(table, queries, starts, *pieces)


def plan_kernel(bias_heads, place_ref, length_ref, order_ref, bias_ref, inverse_ref, angle_ref, start_ref, bias_out, table_ref):
    x, core = place_ref[2], place_ref[3]
    begins, end = [], 0
    for j in range(length_ref.shape[0]):
        begins.append(end)
        end = end + length_ref[j]

    def start_of(position):
        found = jnp.zeros_like(position)
        for begin in begins[1:]:
            found = jnp.where(begin <= position, begin, found)
        return found

    blocks = [order_ref[2 * x + core], order_ref[2 * x + 1 - core]]
    for half, block in enumerate(blocks):
        rows = slice(half * BLOCK, (half + 1) * BLOCK)
        position = block * BLOCK + lax.broadcasted_iota(jnp.int32, (BLOCK, HEAD_DIM), 0)
        start = start_of(position)
        angle_ref[rows, :] = (position - start).astype(jnp.float32) * inverse_ref[...]
        start_ref[rows, :] = start[:, :1]
    first = core == 0
    for at, (zero, one) in enumerate(zip(*bias_heads)):
        bias_out[:, at * HEAD_DIM : (at + 1) * HEAD_DIM] = jnp.where(
            first,
            bias_ref[:, zero * HEAD_DIM : (zero + 1) * HEAD_DIM].astype(jnp.float32),
            bias_ref[:, one * HEAD_DIM : (one + 1) * HEAD_DIM].astype(jnp.float32),
        )
    for slot in range(BLOCKS):
        holder = 2 * lax.rem(x + RING - slot // 2, RING) + lax.rem(core + slot % 2, 2)
        table_ref[order_ref[holder]] = slot
    lowest = BLOCKS
    for step in range(2 * TILES):
        block = blocks[1] if step < TILES else blocks[0]
        row = block * BLOCK + step % TILES * TILE_Q
        low = start_of(row)
        lowest = jnp.minimum(lowest, low // BLOCK)
        table_ref[TABLE_BLOCK + step] = block
        table_ref[TABLE_LOW + step] = low
        table_ref[TABLE_HIGH + step] = start_of(row + TILE_Q - 1)
    table_ref[TABLE_RANGE] = lowest
    table_ref[TABLE_RANGE + 1] = jnp.maximum(blocks[0], blocks[1]) + 1
    table_ref[TABLE_CORE] = core


def plan(place, lengths, order, bias, inverse, bias_heads):
    vmem = pl.BlockSpec(memory_space=pltpu.VMEM)
    return pl.pallas_call(
        functools.partial(plan_kernel, bias_heads),
        grid_spec=pltpu.PrefetchScalarGridSpec(
            num_scalar_prefetch=3,
            grid=(1,),
            in_specs=[vmem] * 2,
            out_specs=[vmem] * 3 + [pl.BlockSpec(memory_space=pltpu.SMEM)],
        ),
        out_shape=[
            jax.ShapeDtypeStruct((2 * BLOCK, HEAD_DIM), jnp.float32),
            jax.ShapeDtypeStruct((2 * BLOCK, 1), jnp.int32),
            jax.ShapeDtypeStruct((1, len(bias_heads[0]) * HEAD_DIM), jnp.float32),
            jax.ShapeDtypeStruct((TABLE_CORE + 1,), jnp.int32),
        ],
        compiler_params=pltpu.CompilerParams(vmem_limit_bytes=VMEM),
    )(place, lengths, order, bias, inverse)


def body(hidden, w_qkv, bias_qkv, doc_lengths, span_order):
    x, core = lax.axis_index("x"), lax.axis_index("core")
    place = jnp.stack([lax.axis_index("y"), lax.axis_index("z"), x, core]).astype(jnp.int32)

    heads = [[HEADS_Q + g, HEADS_Q + KV_HEADS + g] + [g * PER_KV + i for i in range(PER_KV)] for g in range(KV_HEADS)]
    heads_of = [heads[g][:2] + heads[1 - g][:2] + heads[g][2:] + heads[1 - g][2:] for g in range(KV_HEADS)]
    chunk = arrange(place, w_qkv, heads_of)
    kv, columns = 2 * HEAD_DIM, w_qkv.shape[1]
    chunks = around(chunk, lambda a, d: shift(a, "x", d))

    group = jnp.arange(GROUP, dtype=jnp.int32)
    in_slot = group % SLOT
    source = (
        (group % (GROUP // 2)) // SLOT * (2 * SLOT)
        + (x + RING - in_slot // CORE_ROWS) % RING * (2 * CORE_ROWS)
        + group // (GROUP // 2) * CORE_ROWS
        + in_slot % CORE_ROWS
    )
    own = permute_columns(source[None].astype(jnp.int32), after(hidden[0], chunk))
    slot = stack(chunks)
    slot, own, bias_qkv, doc_lengths, span_order = lax.optimization_barrier(
        (slot, own, bias_qkv, doc_lengths, span_order)
    )
    early = around(slot, lambda a, d: shift_by_core(a, EARLY, d))
    partner = swap_cores(own)

    half = HEAD_DIM // 2
    inverse = ROPE_BASE ** (-(jnp.arange(half).astype(jnp.float32) * 2.0) / HEAD_DIM)
    angles, start_column, bias, table = plan(
        place, doc_lengths[0], span_order[0], bias_qkv[None], jnp.concatenate([inverse, inverse])[None], heads
    )
    sign = jnp.where(jnp.arange(HEAD_DIM) < half, -1.0, 1.0)
    cosine, sine = jnp.cos(angles), jnp.sin(angles) * sign[None]
    early[0], bias, cosine, sine, table, start_column = lax.optimization_barrier(
        (early[0], bias, cosine, sine, table, start_column)
    )
    kv_block, q_block = place_rows(early, (0, 2 * kv, columns))
    kv_pieces = gather_direct(kv_block)
    q_block = after(q_block, *kv_pieces[0])
    q_near = gather_near(q_block)
    pairs = project(place, own, partner, bias[:, :kv], cosine, sine, kv_pieces, 1)
    first, third = shift(pairs, "x", 1), shift(pairs, "x", -1)
    far = shift(first[:, :HEAD_DIM], "x", 1), shift(third[:, HEAD_DIM:], "x", -1)
    all_pairs = [pairs, first, *far, third]
    q_near = lax.optimization_barrier((*q_near, pairs))[:2]
    q_pieces = gather_far(q_block, *q_near, (first, third))
    queries = project(place, own, partner, bias[:, kv:], cosine, sine, q_pieces, PER_KV)
    their_rows, result = attend(table, queries, start_column, all_pairs)
    at = (1 - core) * (PER_KV * HEAD_DIM)
    return lax.dynamic_update_slice(result, swap_cores(their_rows), (0, at))[None]


def solution(mesh):
    fine = Mesh(mesh.devices.reshape(RING, RING, RING, 2), ("y", "z", "x", "core"))
    rows = P(("y", "z"), ("x", "core"), None)
    in_specs = (rows, P(("y", "z", "x", "core"), None), P(), P(("y", "z"), None), P(("y", "z"), None))
    return jax.shard_map(body, mesh=fine, in_specs=in_specs, out_specs=rows, check_vma=False)
```

```python
import functools
import itertools
import math

import jax
import jax.numpy as jnp
import numpy as np
from jax import lax
from jax.experimental import pallas as pl
from jax.experimental.pallas import tpu as pltpu
from jax.sharding import Mesh, PartitionSpec as P

HEADS_Q = 14
KV_HEADS = 2
HEAD_DIM = 128
PER_KV = HEADS_Q // KV_HEADS
BLOCK = 512
BLOCKS = 8
RING = 4
CORE_ROWS = 28
SLOT = RING * CORE_ROWS
GROUP = 2 * RING * SLOT
WIDE = 512
PART = 256
TABLE_BLOCK = BLOCKS
TABLE_LOW = TABLE_BLOCK + 2
TABLE_HIGH = TABLE_LOW + 2
TABLE_RANGE = TABLE_HIGH + 2
TABLE_CORE = TABLE_RANGE + 2
ROPE_BASE = 1000000.0
MASKED = -2e38
EXP_SCALE = math.log2(math.e) / math.sqrt(HEAD_DIM)
MIB = 1 << 20
VMEM = 24 * MIB
VMEM_ATTEND = 40 * MIB


def shift(block, axis, distance):
    return lax.ppermute(block, axis, [(i, (i + distance) % RING) for i in range(RING)])


def swap_cores(block):
    return lax.ppermute(block, "core", [(0, 1), (1, 0)])


def shift_by_core(block, axes, distance):
    route = []
    for y, z, x, core in itertools.product(range(RING), range(RING), range(RING), range(2)):
        at = {"y": y, "z": z}
        to = dict(at)
        to[axes[core]] = (at[axes[core]] + distance) % RING
        source = ((y * RING + z) * RING + x) * 2 + core
        route.append((source, ((to["y"] * RING + to["z"]) * RING + x) * 2 + core))
    return lax.ppermute(block, ("y", "z", "x", "core"), route)


def around(block, move):
    return [block, move(block, 1), move(block, 2), move(block, -1)]


EARLY, LATE = ("z", "y"), ("y", "z")


def after(value, *others):
    return lax.optimization_barrier((value, *others))[0]


def gather_direct(block):
    mine = around(block, lambda a, d: shift_by_core(a, LATE, d))
    return mine, [swap_cores(piece) for piece in mine]


def gather_near(block):
    return shift_by_core(block, LATE, 1), shift_by_core(block, LATE, -1)


def gather_far(first, third):
    n = first.shape[1] // 2
    return shift_by_core(first[:, :n], LATE, 1), shift_by_core(third[:, n:], LATE, -1)


def arrange_kernel(heads_of, place_ref, weight_ref, out_ref):
    first = place_ref[3] == 0
    for at, (zero, one) in enumerate(zip(*heads_of)):
        out_ref[:, at * HEAD_DIM : (at + 1) * HEAD_DIM] = jnp.where(
            first,
            weight_ref[:, zero * HEAD_DIM : (zero + 1) * HEAD_DIM],
            weight_ref[:, one * HEAD_DIM : (one + 1) * HEAD_DIM],
        )


def arrange(place, array, heads_of):
    spec = pl.BlockSpec(array.shape, lambda i, place: (0, 0))
    return pl.pallas_call(
        functools.partial(arrange_kernel, heads_of),
        grid_spec=pltpu.PrefetchScalarGridSpec(num_scalar_prefetch=1, grid=(1,), in_specs=[spec], out_specs=spec),
        out_shape=jax.ShapeDtypeStruct(array.shape, array.dtype),
        compiler_params=pltpu.CompilerParams(vmem_limit_bytes=VMEM),
    )(place, array)


def stack_kernel(*refs):
    parts, out = refs[:RING], refs[RING]
    out[...] = jnp.concatenate([part[...] for part in parts], axis=0)


def stack(parts):
    rows, width = parts[0].shape
    whole = pl.BlockSpec((rows, width), lambda i: (0, 0))
    return pl.pallas_call(
        stack_kernel,
        grid=(1,),
        in_specs=[whole] * RING,
        out_specs=pl.BlockSpec((RING * rows, width), lambda i: (0, 0)),
        out_shape=jax.ShapeDtypeStruct((RING * rows, width), parts[0].dtype),
        compiler_params=pltpu.CompilerParams(vmem_limit_bytes=VMEM),
    )(*parts)


def place_kernel(cuts, *refs):
    parts, outs, sems = refs[:RING], refs[RING:-1], refs[-1]
    rows = parts[0].shape[0]
    copies = [
        pltpu.make_async_copy(
            part.at[:, pl.ds(a, b - a)], out.at[pl.ds(i * rows, rows), :], sems.at[n, i]
        )
        for n, (out, a, b) in enumerate(zip(outs, cuts, cuts[1:]))
        for i, part in enumerate(parts)
    ]
    for copy in copies:
        copy.start()
    for copy in copies:
        copy.wait()


def place_rows(parts, cuts):
    rows = RING * parts[0].shape[0]
    shapes = [(rows, b - a) for a, b in zip(cuts, cuts[1:])]
    return pl.pallas_call(
        functools.partial(place_kernel, cuts),
        grid=(1,),
        in_specs=[pl.BlockSpec(memory_space=pl.ANY)] * RING,
        out_specs=[pl.BlockSpec(shape, lambda i: (0, 0)) for shape in shapes],
        out_shape=[jax.ShapeDtypeStruct(shape, parts[0].dtype) for shape in shapes],
        scratch_shapes=[pltpu.SemaphoreType.DMA((len(shapes), RING))],
        compiler_params=pltpu.CompilerParams(vmem_limit_bytes=VMEM),
    )(*parts)


def permute_kernel(place_ref, source_ref, rows_ref, out_ref, matrix):
    row = lax.broadcasted_iota(jnp.int32, matrix.shape, 0)
    matrix[...] = jnp.where(row == source_ref[...], 1.0, 0.0).astype(jnp.bfloat16)
    half = GROUP // 2
    parts = [[] for _ in range(RING)]
    for behind in range(RING):
        at = lax.rem(place_ref[0] + RING - behind, RING) * GROUP
        moved = jnp.dot(
            rows_ref[:, pl.ds(pl.multiple_of(at, GROUP), GROUP)], matrix[...], preferred_element_type=jnp.float32
        )
        out_ref[:, behind * WIDE : behind * WIDE + half] = moved[:, :half].astype(jnp.bfloat16)
        for slot in range(RING):
            parts[slot].append(moved[:, half + slot * SLOT : half + (slot + 1) * SLOT])
    for slot in range(RING):
        start = (RING + slot) * WIDE
        out_ref[:, start : start + half] = jnp.concatenate(parts[slot], axis=1).astype(jnp.bfloat16)


def permute_columns(place, source, rows):
    vmem = pl.BlockSpec(memory_space=pltpu.VMEM)
    return pl.pallas_call(
        permute_kernel,
        grid_spec=pltpu.PrefetchScalarGridSpec(
            num_scalar_prefetch=1,
            grid=(1,),
            in_specs=[vmem, vmem],
            out_specs=vmem,
            scratch_shapes=[pltpu.VMEM((GROUP, GROUP), jnp.bfloat16)],
        ),
        out_shape=jax.ShapeDtypeStruct((rows.shape[0], 2 * RING * WIDE), jnp.bfloat16),
        compiler_params=pltpu.CompilerParams(vmem_limit_bytes=VMEM),
    )(place, source, rows)


def project_kernel(terms, columns, rotated, add, finish, place_ref, own_ref, partner_ref, *refs):
    pieces, refs = refs[: len(terms)], refs[len(terms) :]
    out_ref = refs[-1]
    core = place_ref[3]
    half = GROUP // 2
    for side, rows_ref in enumerate((own_ref, partner_ref)):
        rows = slice(side * BLOCK, (side + 1) * BLOCK)
        total = refs[0][rows] if add else None
        for (family, behind, row, column), piece in zip(terms, pieces):
            part = core if family == 0 else 1 - core
            at = pl.multiple_of((part * RING + behind) * WIDE, WIDE)
            product = jnp.dot(
                rows_ref[:, pl.ds(at, WIDE)][:, :half],
                piece[row : row + half, column : column + columns],
                preferred_element_type=jnp.float32,
            )
            total = product if total is None else total + product
        if not finish:
            out_ref[rows] = total
            continue
        bias_ref, cos_ref, sin_ref = refs[-4:-1]
        total = total + bias_ref[...]
        cosine, sine = cos_ref[rows], sin_ref[rows]
        for head in range(columns // HEAD_DIM):
            lanes = slice(head * HEAD_DIM, (head + 1) * HEAD_DIM)
            one = total[:, lanes]
            if head < rotated:
                one = one * cosine + pltpu.roll(one, HEAD_DIM // 2, 1) * sine
            out_ref[rows, lanes] = one.astype(jnp.bfloat16)


def project(place, own, partner, pieces, columns, partial=None, ends=None, rotated=0):
    vmem = pl.BlockSpec(memory_space=pltpu.VMEM)
    more = ([] if partial is None else [partial]) + list(ends or ())
    return pl.pallas_call(
        functools.partial(
            project_kernel, [p[1:] for p in pieces], columns, rotated, partial is not None, ends is not None
        ),
        grid_spec=pltpu.PrefetchScalarGridSpec(
            num_scalar_prefetch=1,
            grid=(1,),
            in_specs=[vmem] * (2 + len(pieces) + len(more)),
            out_specs=vmem,
        ),
        out_shape=jax.ShapeDtypeStruct((2 * BLOCK, columns), jnp.bfloat16 if ends else jnp.float32),
        compiler_params=pltpu.CompilerParams(vmem_limit_bytes=VMEM),
    )(place, own, partner, *[p[0] for p in pieces], *more)


def attend_kernel(heads, table_ref, query_ref, start_ref, *refs):
    pieces = refs[: RING + 1]
    their_ref, my_ref, kept, stacked, maxima, totals, summed, sems = refs[RING + 1 :]
    step = pl.program_id(0)
    block = table_ref[TABLE_BLOCK + step]
    low = table_ref[TABLE_LOW + step]
    high = table_ref[TABLE_HIGH + step]

    def each_block(act):
        def one(b, carry):
            slot = table_ref[b]
            for s in range(BLOCKS):

                @pl.when(slot == s)
                def _():
                    rows = pl.ds((s % 2) * BLOCK, BLOCK)
                    if s // 2 == 2:
                        for n in range(2):
                            act(
                                pltpu.make_async_copy(
                                    pieces[2 + n].at[rows, :],
                                    kept.at[b, :, pl.ds(n * HEAD_DIM, HEAD_DIM)],
                                    sems.at[n, b],
                                )
                            )
                    else:
                        piece = pieces[s // 2 if s // 2 < 2 else RING]
                        act(pltpu.make_async_copy(piece.at[rows, :], kept.at[b], sems.at[0, b]))

            return carry

        lax.fori_loop(table_ref[TABLE_RANGE], table_ref[TABLE_RANGE + 1], one, 0)

    @pl.when(step == 0)
    def _():
        each_block(lambda copy: copy.start())

    rows, lead = heads * BLOCK, heads * PART
    for part in range(2):
        for head in range(heads):
            at = (part * heads + head) * PART
            stacked[at : at + PART] = query_ref[part * PART : (part + 1) * PART, head * HEAD_DIM : (head + 1) * HEAD_DIM]
    starts = start_ref[...] - block * BLOCK

    @pl.when(step == 0)
    def _():
        each_block(lambda copy: copy.wait())

    def lanes(values_in):
        return [values_in[:, i * HEAD_DIM : (i + 1) * HEAD_DIM] for i in range(values_in.shape[1] // HEAD_DIM)]

    def score(of, key_tile, visible):
        found = lax.dot_general(
            stacked[of], key_tile, (((1,), (1,)), ((), ())), preferred_element_type=jnp.float32
        )
        if visible is None:
            return found
        count, keys = visible.shape[0] // PART, visible.shape[1]
        visible = visible.reshape(count, 1, PART, keys)
        return jnp.where(visible, found.reshape(count, heads, PART, keys), MASKED).reshape(found.shape)

    def weigh(found, top):
        weights = [jnp.exp2((part - top) * EXP_SCALE) for part in lanes(found)]
        rounded = jnp.concatenate([w.astype(jnp.bfloat16) for w in weights], axis=1)
        return functools.reduce(jnp.add, weights), rounded

    for part in range(2):
        of, count = slice(part * lead, (part + 1) * lead), (part + 1) * PART
        key = lax.broadcasted_iota(jnp.int32, (PART, count), 1)
        row = part * PART + lax.broadcasted_iota(jnp.int32, (PART, count), 0)
        visible = (key >= starts[part * PART : (part + 1) * PART]) & (key <= row)
        found = score(of, kept[block, :count, :HEAD_DIM], visible)
        top = jnp.max(functools.reduce(jnp.maximum, lanes(found)), axis=1, keepdims=True)
        top = jnp.broadcast_to(top, (lead, HEAD_DIM))
        maxima[of] = top
        totals[of], rounded = weigh(found, top)
        summed[of] = jnp.dot(rounded, kept[block, :count, HEAD_DIM:], preferred_element_type=jnp.float32)

    def visit(t, masked):
        visible = None
        if masked:
            key = (t - block) * BLOCK + lax.broadcasted_iota(jnp.int32, (BLOCK, BLOCK), 1)
            visible = key >= starts
        found = score(slice(0, rows), kept[t, :, :HEAD_DIM], visible)
        before = maxima[...]
        top = functools.reduce(jnp.maximum, lanes(found))
        top = jnp.maximum(before, jnp.max(top, axis=1, keepdims=True))
        factor = jnp.exp2((before - top) * EXP_SCALE)
        maxima[...] = top
        added, rounded = weigh(found, top)
        totals[...] = totals[...] * factor + added
        summed[...] = summed[...] * factor + jnp.dot(
            rounded, kept[t, :, HEAD_DIM:], preferred_element_type=jnp.float32
        )

    def one_tile(t, carry):
        whole = t * BLOCK >= high

        @pl.when(whole)
        def _():
            visit(t, False)

        @pl.when(jnp.logical_not(whole))
        def _():
            visit(t, True)

        return carry

    lax.fori_loop(low // BLOCK, block, one_tile, 0)

    def store(out_ref):
        result = (summed[...] / jnp.sum(totals[...], axis=1, keepdims=True)).astype(jnp.bfloat16)
        for part in range(2):
            for head in range(heads):
                at = (part * heads + head) * PART
                out_ref[part * PART : (part + 1) * PART, head * HEAD_DIM : (head + 1) * HEAD_DIM] = result[at : at + PART]

    @pl.when(step == 0)
    def _():
        store(their_ref)

    @pl.when(step == 1)
    def _():
        store(my_ref)


def attend(table, queries, starts, pieces):
    heads = queries.shape[1] // HEAD_DIM

    def rows_of(width):
        return pl.BlockSpec((BLOCK, width), lambda i, table: (1 - i, 0))

    wide = (BLOCK, heads * HEAD_DIM)
    return pl.pallas_call(
        functools.partial(attend_kernel, heads),
        grid_spec=pltpu.PrefetchScalarGridSpec(
            num_scalar_prefetch=1,
            grid=(2,),
            in_specs=[rows_of(heads * HEAD_DIM), rows_of(1)] + [pl.BlockSpec(memory_space=pl.ANY)] * (RING + 1),
            out_specs=[
                pl.BlockSpec(wide, lambda i, table: (0, 0)),
                pl.BlockSpec(wide, lambda i, table: (0, table[TABLE_CORE])),
            ],
            scratch_shapes=[
                pltpu.VMEM((BLOCKS, BLOCK, 2 * HEAD_DIM), jnp.bfloat16),
                pltpu.VMEM((heads * BLOCK, HEAD_DIM), jnp.bfloat16),
                pltpu.VMEM((heads * BLOCK, HEAD_DIM), jnp.float32),
                pltpu.VMEM((heads * BLOCK, HEAD_DIM), jnp.float32),
                pltpu.VMEM((heads * BLOCK, HEAD_DIM), jnp.float32),
                pltpu.SemaphoreType.DMA((2, BLOCKS)),
            ],
        ),
        out_shape=[
            jax.ShapeDtypeStruct((BLOCK, heads * HEAD_DIM), jnp.bfloat16),
            jax.ShapeDtypeStruct((BLOCK, KV_HEADS * heads * HEAD_DIM), jnp.bfloat16),
        ],
        compiler_params=pltpu.CompilerParams(vmem_limit_bytes=VMEM_ATTEND),
    )(table, queries, starts, *pieces)


def plan_kernel(bias_heads, place_ref, length_ref, order_ref, bias_ref, inverse_ref, angle_ref, start_ref, bias_out, table_ref):
    x, core = place_ref[2], place_ref[3]
    begins, end = [], 0
    for j in range(length_ref.shape[0]):
        begins.append(end)
        end = end + length_ref[j]

    def start_of(position):
        found = jnp.zeros_like(position)
        for begin in begins[1:]:
            found = jnp.where(begin <= position, begin, found)
        return found

    blocks = [order_ref[2 * x + core], order_ref[2 * x + 1 - core]]
    for half, block in enumerate(blocks):
        rows = slice(half * BLOCK, (half + 1) * BLOCK)
        position = block * BLOCK + lax.broadcasted_iota(jnp.int32, (BLOCK, HEAD_DIM), 0)
        start = start_of(position)
        angle_ref[rows, :] = (position - start).astype(jnp.float32) * inverse_ref[...]
        start_ref[rows, :] = start[:, :1]
    first = core == 0
    for at, (zero, one) in enumerate(zip(*bias_heads)):
        bias_out[:, at * HEAD_DIM : (at + 1) * HEAD_DIM] = jnp.where(
            first,
            bias_ref[:, zero * HEAD_DIM : (zero + 1) * HEAD_DIM].astype(jnp.float32),
            bias_ref[:, one * HEAD_DIM : (one + 1) * HEAD_DIM].astype(jnp.float32),
        )
    for slot in range(BLOCKS):
        holder = 2 * lax.rem(x + RING - slot // 2, RING) + lax.rem(core + slot % 2, 2)
        table_ref[order_ref[holder]] = slot
    lowest = BLOCKS
    for step in range(2):
        block = blocks[1 - step]
        row = block * BLOCK
        low = start_of(row)
        lowest = jnp.minimum(lowest, low // BLOCK)
        table_ref[TABLE_BLOCK + step] = block
        table_ref[TABLE_LOW + step] = low
        table_ref[TABLE_HIGH + step] = start_of(row + BLOCK - 1)
    table_ref[TABLE_RANGE] = lowest
    table_ref[TABLE_RANGE + 1] = jnp.maximum(blocks[0], blocks[1]) + 1
    table_ref[TABLE_CORE] = core


def plan(place, lengths, order, bias, inverse, bias_heads):
    vmem = pl.BlockSpec(memory_space=pltpu.VMEM)
    return pl.pallas_call(
        functools.partial(plan_kernel, bias_heads),
        grid_spec=pltpu.PrefetchScalarGridSpec(
            num_scalar_prefetch=3,
            grid=(1,),
            in_specs=[vmem] * 2,
            out_specs=[vmem] * 3 + [pl.BlockSpec(memory_space=pltpu.SMEM)],
        ),
        out_shape=[
            jax.ShapeDtypeStruct((2 * BLOCK, HEAD_DIM), jnp.float32),
            jax.ShapeDtypeStruct((2 * BLOCK, 1), jnp.int32),
            jax.ShapeDtypeStruct((1, len(bias_heads[0]) * HEAD_DIM), jnp.float32),
            jax.ShapeDtypeStruct((TABLE_CORE + 1,), jnp.int32),
        ],
        compiler_params=pltpu.CompilerParams(vmem_limit_bytes=VMEM),
    )(place, lengths, order, bias, inverse)


def body(hidden, w_qkv, bias_qkv, doc_lengths, span_order):
    x, core = lax.axis_index("x"), lax.axis_index("core")
    y, z = lax.axis_index("y"), lax.axis_index("z")
    place = jnp.stack([y, z, x, core]).astype(jnp.int32)

    heads = [[HEADS_Q + g, HEADS_Q + KV_HEADS + g] + [g * PER_KV + i for i in range(PER_KV)] for g in range(KV_HEADS)]
    heads_of = [heads[g][:2] + heads[1 - g][:2] + heads[g][2:] + heads[1 - g][2:] for g in range(KV_HEADS)]
    chunk = arrange(place, w_qkv, heads_of)
    kv, columns = 2 * HEAD_DIM, w_qkv.shape[1]
    chunks = around(chunk, lambda a, d: shift(a, "x", d))

    group = jnp.arange(GROUP, dtype=jnp.int32)
    in_slot = group % SLOT
    source = (
        (z + RING - (group % (GROUP // 2)) // SLOT) % RING * (2 * SLOT)
        + (x + RING - in_slot // CORE_ROWS) % RING * (2 * CORE_ROWS)
        + group // (GROUP // 2) * CORE_ROWS
        + in_slot % CORE_ROWS
    )
    own = permute_columns(place, source[None].astype(jnp.int32), after(hidden[0], chunk))
    slot = stack(chunks)
    slot, own, bias_qkv, doc_lengths, span_order = lax.optimization_barrier(
        (slot, own, bias_qkv, doc_lengths, span_order)
    )
    early = around(slot, lambda a, d: shift_by_core(a, EARLY, d))
    partner = swap_cores(own)

    half = HEAD_DIM // 2
    inverse = ROPE_BASE ** (-(jnp.arange(half).astype(jnp.float32) * 2.0) / HEAD_DIM)
    angles, start_column, bias, table = plan(
        place, doc_lengths[0], span_order[0], bias_qkv[None], jnp.concatenate([inverse, inverse])[None], heads
    )
    sign = jnp.where(jnp.arange(HEAD_DIM) < half, -1.0, 1.0)
    cosine, sine = jnp.cos(angles), jnp.sin(angles) * sign[None]
    early[0], bias, cosine, sine, table, start_column = lax.optimization_barrier(
        (early[0], bias, cosine, sine, table, start_column)
    )
    kv_block, q_block = place_rows(early, (0, 2 * kv, columns))
    kv_pieces = gather_direct(kv_block)
    q_block = after(q_block, *kv_pieces[0])
    q_near = gather_near(q_block)
    kv_terms = [(a, 0, d, 0, 0) for d, a in enumerate(kv_pieces[0])]
    kv_terms += [(a, 1, d, 0, kv) for d, a in enumerate(kv_pieces[1])]
    pairs = project(place, own, partner, kv_terms, kv, ends=(bias[:, :kv], cosine, sine), rotated=1)
    first, third = shift(pairs, "x", 1), shift(pairs, "x", -1)
    far = shift(first[:, :HEAD_DIM], "x", 1), shift(third[:, HEAD_DIM:], "x", -1)
    all_pairs = [pairs, first, *far, third]

    n = PER_KV * HEAD_DIM
    q_first, q_third = lax.optimization_barrier((*q_near, pairs))[:2]
    q_mine, q_other = gather_far(q_first, q_third)
    near_other = jnp.concatenate([q_block[:, n:], q_first[:, n:], q_third[:, n:]], axis=0)
    near_other = swap_cores(after(near_other, pairs))
    near = [(q_block, 0, 0, 0, 0), (q_first, 0, 1, 0, 0), (q_third, 0, 3, 0, 0)]
    near += [(near_other, 1, d, i * (GROUP // 2), 0) for i, d in enumerate((0, 1, 3))]
    partial = project(place, own, partner, near, n)
    q_other, q_mine = lax.optimization_barrier((q_other, q_mine, first, third, partial))[:2]
    last = [(q_mine, 0, 2, 0, 0), (swap_cores(q_other), 1, 2, 0, 0)]
    queries = project(place, own, partner, last, n, partial, (bias[:, kv:], cosine, sine), PER_KV)
    their_rows, result = attend(table, queries, start_column, all_pairs)
    at = (1 - core) * (PER_KV * HEAD_DIM)
    return lax.dynamic_update_slice(result, swap_cores(their_rows), (0, at))[None]


def solution(mesh):
    fine = Mesh(mesh.devices.reshape(RING, RING, RING, 2), ("y", "z", "x", "core"))
    rows = P(("y", "z"), ("x", "core"), None)
    in_specs = (rows, P(("y", "z", "x", "core"), None), P(), P(("y", "z"), None), P(("y", "z"), None))
    return jax.shard_map(body, mesh=fine, in_specs=in_specs, out_specs=rows, check_vma=False)
```

```python
import functools
import itertools
import math

import jax
import jax.numpy as jnp
import numpy as np
from jax import lax
from jax.experimental import pallas as pl
from jax.experimental.pallas import tpu as pltpu
from jax.sharding import Mesh, PartitionSpec as P

HEADS_Q = 14
KV_HEADS = 2
HEAD_DIM = 128
PER_KV = HEADS_Q // KV_HEADS
BLOCK = 512
BLOCKS = 8
RING = 4
CORE_ROWS = 28
SLOT = RING * CORE_ROWS
GROUP = 2 * RING * SLOT
WIDE = 512
PART = 256
TABLE_BLOCK = BLOCKS
TABLE_LOW = TABLE_BLOCK + 2
TABLE_HIGH = TABLE_LOW + 2
TABLE_RANGE = TABLE_HIGH + 2
TABLE_CORE = TABLE_RANGE + 2
ROPE_BASE = 1000000.0
MASKED = -2e38
EXP_SCALE = math.log2(math.e) / math.sqrt(HEAD_DIM)
MIB = 1 << 20
VMEM = 24 * MIB
VMEM_ATTEND = 40 * MIB


def shift(block, axis, distance):
    return lax.ppermute(block, axis, [(i, (i + distance) % RING) for i in range(RING)])


def swap_cores(block):
    return lax.ppermute(block, "core", [(0, 1), (1, 0)])


def shift_by_core(block, axes, distance):
    route = []
    for y, z, x, core in itertools.product(range(RING), range(RING), range(RING), range(2)):
        at = {"y": y, "z": z}
        to = dict(at)
        to[axes[core]] = (at[axes[core]] + distance) % RING
        source = ((y * RING + z) * RING + x) * 2 + core
        route.append((source, ((to["y"] * RING + to["z"]) * RING + x) * 2 + core))
    return lax.ppermute(block, ("y", "z", "x", "core"), route)


def around(block, move):
    return [block, move(block, 1), move(block, 2), move(block, -1)]


EARLY, LATE = ("z", "y"), ("y", "z")


def after(value, *others):
    return lax.optimization_barrier((value, *others))[0]


def gather_direct(block):
    mine = around(block, lambda a, d: shift_by_core(a, LATE, d))
    return mine, [swap_cores(piece) for piece in mine]


def gather_near(block):
    return shift_by_core(block, LATE, 1), shift_by_core(block, LATE, -1)


def gather_far(first, third):
    n = first.shape[1] // 2
    return shift_by_core(first[:, :n], LATE, 1), shift_by_core(third[:, n:], LATE, -1)


def arrange_kernel(heads_of, place_ref, weight_ref, out_ref):
    first = place_ref[3] == 0
    for at, (zero, one) in enumerate(zip(*heads_of)):
        out_ref[:, at * HEAD_DIM : (at + 1) * HEAD_DIM] = jnp.where(
            first,
            weight_ref[:, zero * HEAD_DIM : (zero + 1) * HEAD_DIM],
            weight_ref[:, one * HEAD_DIM : (one + 1) * HEAD_DIM],
        )


def arrange(place, array, heads_of):
    spec = pl.BlockSpec(array.shape, lambda i, place: (0, 0))
    return pl.pallas_call(
        functools.partial(arrange_kernel, heads_of),
        grid_spec=pltpu.PrefetchScalarGridSpec(num_scalar_prefetch=1, grid=(1,), in_specs=[spec], out_specs=spec),
        out_shape=jax.ShapeDtypeStruct(array.shape, array.dtype),
        compiler_params=pltpu.CompilerParams(vmem_limit_bytes=VMEM),
    )(place, array)


def stack_kernel(*refs):
    parts, out = refs[:RING], refs[RING]
    out[...] = jnp.concatenate([part[...] for part in parts], axis=0)


def stack(parts):
    rows, width = parts[0].shape
    whole = pl.BlockSpec((rows, width), lambda i: (0, 0))
    return pl.pallas_call(
        stack_kernel,
        grid=(1,),
        in_specs=[whole] * RING,
        out_specs=pl.BlockSpec((RING * rows, width), lambda i: (0, 0)),
        out_shape=jax.ShapeDtypeStruct((RING * rows, width), parts[0].dtype),
        compiler_params=pltpu.CompilerParams(vmem_limit_bytes=VMEM),
    )(*parts)


def place_kernel(cuts, *refs):
    parts, outs, sems = refs[:RING], refs[RING:-1], refs[-1]
    rows = parts[0].shape[0]
    copies = [
        pltpu.make_async_copy(
            part.at[:, pl.ds(a, b - a)], out.at[pl.ds(i * rows, rows), :], sems.at[n, i]
        )
        for n, (out, a, b) in enumerate(zip(outs, cuts, cuts[1:]))
        for i, part in enumerate(parts)
    ]
    for copy in copies:
        copy.start()
    for copy in copies:
        copy.wait()


def place_rows(parts, cuts):
    rows = RING * parts[0].shape[0]
    shapes = [(rows, b - a) for a, b in zip(cuts, cuts[1:])]
    return pl.pallas_call(
        functools.partial(place_kernel, cuts),
        grid=(1,),
        in_specs=[pl.BlockSpec(memory_space=pl.ANY)] * RING,
        out_specs=[pl.BlockSpec(shape, lambda i: (0, 0)) for shape in shapes],
        out_shape=[jax.ShapeDtypeStruct(shape, parts[0].dtype) for shape in shapes],
        scratch_shapes=[pltpu.SemaphoreType.DMA((len(shapes), RING))],
        compiler_params=pltpu.CompilerParams(vmem_limit_bytes=VMEM),
    )(*parts)


def permute_kernel(place_ref, source_ref, rows_ref, out_ref, matrix):
    row = lax.broadcasted_iota(jnp.int32, matrix.shape, 0)
    matrix[...] = jnp.where(row == source_ref[...], 1.0, 0.0).astype(jnp.bfloat16)
    half = GROUP // 2
    parts = [[] for _ in range(RING)]
    for behind in range(RING):
        at = lax.rem(place_ref[0] + RING - behind, RING) * GROUP
        moved = jnp.dot(
            rows_ref[:, pl.ds(pl.multiple_of(at, GROUP), GROUP)], matrix[...], preferred_element_type=jnp.float32
        )
        out_ref[:, behind * WIDE : behind * WIDE + half] = moved[:, :half].astype(jnp.bfloat16)
        for slot in range(RING):
            parts[slot].append(moved[:, half + slot * SLOT : half + (slot + 1) * SLOT])
    for slot in range(RING):
        start = (RING + slot) * WIDE
        out_ref[:, start : start + half] = jnp.concatenate(parts[slot], axis=1).astype(jnp.bfloat16)


def permute_columns(place, source, rows):
    vmem = pl.BlockSpec(memory_space=pltpu.VMEM)
    return pl.pallas_call(
        permute_kernel,
        grid_spec=pltpu.PrefetchScalarGridSpec(
            num_scalar_prefetch=1,
            grid=(1,),
            in_specs=[vmem, vmem],
            out_specs=vmem,
            scratch_shapes=[pltpu.VMEM((GROUP, GROUP), jnp.bfloat16)],
        ),
        out_shape=jax.ShapeDtypeStruct((rows.shape[0], 2 * RING * WIDE), jnp.bfloat16),
        compiler_params=pltpu.CompilerParams(vmem_limit_bytes=VMEM),
    )(place, source, rows)


def project_kernel(terms, columns, rotated, add, finish, place_ref, own_ref, partner_ref, *refs):
    pieces, refs = refs[: len(terms)], refs[len(terms) :]
    out_ref = refs[-1]
    core = place_ref[3]
    half = GROUP // 2
    for side, rows_ref in enumerate((own_ref, partner_ref)):
        rows = slice(side * BLOCK, (side + 1) * BLOCK)
        total = refs[0][rows] if add else None
        for (family, behind, row, column), piece in zip(terms, pieces):
            part = core if family == 0 else 1 - core
            at = pl.multiple_of((part * RING + behind) * WIDE, WIDE)
            product = jnp.dot(
                rows_ref[:, pl.ds(at, WIDE)][:, :half],
                piece[row : row + half, column : column + columns],
                preferred_element_type=jnp.float32,
            )
            total = product if total is None else total + product
        if not finish:
            out_ref[rows] = total
            continue
        bias_ref, cos_ref, sin_ref = refs[-4:-1]
        total = total + bias_ref[...]
        cosine, sine = cos_ref[rows], sin_ref[rows]
        for head in range(columns // HEAD_DIM):
            lanes = slice(head * HEAD_DIM, (head + 1) * HEAD_DIM)
            one = total[:, lanes]
            if head < rotated:
                one = one * cosine + pltpu.roll(one, HEAD_DIM // 2, 1) * sine
            out_ref[rows, lanes] = one.astype(jnp.bfloat16)


def project(place, own, partner, pieces, columns, partial=None, ends=None, rotated=0):
    vmem = pl.BlockSpec(memory_space=pltpu.VMEM)
    more = ([] if partial is None else [partial]) + list(ends or ())
    return pl.pallas_call(
        functools.partial(
            project_kernel, [p[1:] for p in pieces], columns, rotated, partial is not None, ends is not None
        ),
        grid_spec=pltpu.PrefetchScalarGridSpec(
            num_scalar_prefetch=1,
            grid=(1,),
            in_specs=[vmem] * (2 + len(pieces) + len(more)),
            out_specs=vmem,
        ),
        out_shape=jax.ShapeDtypeStruct((2 * BLOCK, columns), jnp.bfloat16 if ends else jnp.float32),
        compiler_params=pltpu.CompilerParams(vmem_limit_bytes=VMEM),
    )(place, own, partner, *[p[0] for p in pieces], *more)


def attend_kernel(heads, table_ref, query_ref, start_ref, *refs):
    pieces = refs[: RING + 1]
    their_ref, my_ref, kept, stacked, maxima, totals, summed, sems = refs[RING + 1 :]
    step = pl.program_id(0)
    block = table_ref[TABLE_BLOCK + step]
    low = table_ref[TABLE_LOW + step]
    high = table_ref[TABLE_HIGH + step]

    def each_block(act):
        def one(b, carry):
            slot = table_ref[b]
            for s in range(BLOCKS):

                @pl.when(slot == s)
                def _():
                    rows = pl.ds((s % 2) * BLOCK, BLOCK)
                    if s // 2 == 2:
                        for n in range(2):
                            act(
                                pltpu.make_async_copy(
                                    pieces[2 + n].at[rows, :],
                                    kept.at[b, :, pl.ds(n * HEAD_DIM, HEAD_DIM)],
                                    sems.at[n, b],
                                )
                            )
                    else:
                        piece = pieces[s // 2 if s // 2 < 2 else RING]
                        act(pltpu.make_async_copy(piece.at[rows, :], kept.at[b], sems.at[0, b]))

            return carry

        lax.fori_loop(table_ref[TABLE_RANGE], table_ref[TABLE_RANGE + 1], one, 0)

    @pl.when(step == 0)
    def _():
        each_block(lambda copy: copy.start())

    rows, lead = heads * BLOCK, heads * PART
    for part in range(2):
        for head in range(heads):
            at = (part * heads + head) * PART
            stacked[at : at + PART] = query_ref[part * PART : (part + 1) * PART, head * HEAD_DIM : (head + 1) * HEAD_DIM]
    starts = start_ref[...] - block * BLOCK

    @pl.when(step == 0)
    def _():
        each_block(lambda copy: copy.wait())

    def lanes(values_in):
        return [values_in[:, i * HEAD_DIM : (i + 1) * HEAD_DIM] for i in range(values_in.shape[1] // HEAD_DIM)]

    def score(of, key_tile, visible):
        found = lax.dot_general(
            stacked[of], key_tile, (((1,), (1,)), ((), ())), preferred_element_type=jnp.float32
        )
        if visible is None:
            return found
        count, keys = visible.shape[0] // PART, visible.shape[1]
        visible = visible.reshape(count, 1, PART, keys)
        return jnp.where(visible, found.reshape(count, heads, PART, keys), MASKED).reshape(found.shape)

    def weigh(found, top):
        weights = [jnp.exp2((part - top) * EXP_SCALE) for part in lanes(found)]
        rounded = jnp.concatenate([w.astype(jnp.bfloat16) for w in weights], axis=1)
        return functools.reduce(jnp.add, weights), rounded

    for part in range(2):
        of, count = slice(part * lead, (part + 1) * lead), (part + 1) * PART
        key = lax.broadcasted_iota(jnp.int32, (PART, count), 1)
        row = part * PART + lax.broadcasted_iota(jnp.int32, (PART, count), 0)
        visible = (key >= starts[part * PART : (part + 1) * PART]) & (key <= row)
        found = score(of, kept[block, :count, :HEAD_DIM], visible)
        top = jnp.max(functools.reduce(jnp.maximum, lanes(found)), axis=1, keepdims=True)
        top = jnp.broadcast_to(top, (lead, HEAD_DIM))
        maxima[of] = top
        totals[of], rounded = weigh(found, top)
        summed[of] = jnp.dot(rounded, kept[block, :count, HEAD_DIM:], preferred_element_type=jnp.float32)

    def visit(t, masked):
        visible = None
        if masked:
            key = (t - block) * BLOCK + lax.broadcasted_iota(jnp.int32, (BLOCK, BLOCK), 1)
            visible = key >= starts
        found = score(slice(0, rows), kept[t, :, :HEAD_DIM], visible)
        before = maxima[...]
        top = functools.reduce(jnp.maximum, lanes(found))
        top = jnp.maximum(before, jnp.max(top, axis=1, keepdims=True))
        factor = jnp.exp2((before - top) * EXP_SCALE)
        maxima[...] = top
        added, rounded = weigh(found, top)
        totals[...] = totals[...] * factor + added
        summed[...] = summed[...] * factor + jnp.dot(
            rounded, kept[t, :, HEAD_DIM:], preferred_element_type=jnp.float32
        )

    def one_tile(t, carry):
        whole = t * BLOCK >= high

        @pl.when(whole)
        def _():
            visit(t, False)

        @pl.when(jnp.logical_not(whole))
        def _():
            visit(t, True)

        return carry

    lax.fori_loop(low // BLOCK, block, one_tile, 0)

    def store(out_ref):
        result = (summed[...] / jnp.sum(totals[...], axis=1, keepdims=True)).astype(jnp.bfloat16)
        for part in range(2):
            for head in range(heads):
                at = (part * heads + head) * PART
                out_ref[part * PART : (part + 1) * PART, head * HEAD_DIM : (head + 1) * HEAD_DIM] = result[at : at + PART]

    @pl.when(step == 0)
    def _():
        store(their_ref)

    @pl.when(step == 1)
    def _():
        store(my_ref)


def attend(table, queries, starts, pieces):
    heads = queries.shape[1] // HEAD_DIM

    def rows_of(width):
        return pl.BlockSpec((BLOCK, width), lambda i, table: (1 - i, 0))

    wide = (BLOCK, heads * HEAD_DIM)
    return pl.pallas_call(
        functools.partial(attend_kernel, heads),
        grid_spec=pltpu.PrefetchScalarGridSpec(
            num_scalar_prefetch=1,
            grid=(2,),
            in_specs=[rows_of(heads * HEAD_DIM), rows_of(1)] + [pl.BlockSpec(memory_space=pl.ANY)] * (RING + 1),
            out_specs=[
                pl.BlockSpec(wide, lambda i, table: (0, 0)),
                pl.BlockSpec(wide, lambda i, table: (0, table[TABLE_CORE])),
            ],
            scratch_shapes=[
                pltpu.VMEM((BLOCKS, BLOCK, 2 * HEAD_DIM), jnp.bfloat16),
                pltpu.VMEM((heads * BLOCK, HEAD_DIM), jnp.bfloat16),
                pltpu.VMEM((heads * BLOCK, HEAD_DIM), jnp.float32),
                pltpu.VMEM((heads * BLOCK, HEAD_DIM), jnp.float32),
                pltpu.VMEM((heads * BLOCK, HEAD_DIM), jnp.float32),
                pltpu.SemaphoreType.DMA((2, BLOCKS)),
            ],
        ),
        out_shape=[
            jax.ShapeDtypeStruct((BLOCK, heads * HEAD_DIM), jnp.bfloat16),
            jax.ShapeDtypeStruct((BLOCK, KV_HEADS * heads * HEAD_DIM), jnp.bfloat16),
        ],
        compiler_params=pltpu.CompilerParams(vmem_limit_bytes=VMEM_ATTEND),
    )(table, queries, starts, *pieces)


def plan_kernel(bias_heads, place_ref, length_ref, order_ref, bias_ref, inverse_ref, angle_ref, start_ref, bias_out, table_ref):
    x, core = place_ref[2], place_ref[3]
    begins, end = [], 0
    for j in range(length_ref.shape[0]):
        begins.append(end)
        end = end + length_ref[j]

    def start_of(position):
        found = jnp.zeros_like(position)
        for begin in begins[1:]:
            found = jnp.where(begin <= position, begin, found)
        return found

    blocks = [order_ref[2 * x + core], order_ref[2 * x + 1 - core]]
    for half, block in enumerate(blocks):
        rows = slice(half * BLOCK, (half + 1) * BLOCK)
        position = block * BLOCK + lax.broadcasted_iota(jnp.int32, (BLOCK, HEAD_DIM), 0)
        start = start_of(position)
        angle_ref[rows, :] = (position - start).astype(jnp.float32) * inverse_ref[...]
        start_ref[rows, :] = start[:, :1]
    first = core == 0
    for at, (zero, one) in enumerate(zip(*bias_heads)):
        bias_out[:, at * HEAD_DIM : (at + 1) * HEAD_DIM] = jnp.where(
            first,
            bias_ref[:, zero * HEAD_DIM : (zero + 1) * HEAD_DIM].astype(jnp.float32),
            bias_ref[:, one * HEAD_DIM : (one + 1) * HEAD_DIM].astype(jnp.float32),
        )
    for slot in range(BLOCKS):
        holder = 2 * lax.rem(x + RING - slot // 2, RING) + lax.rem(core + slot % 2, 2)
        table_ref[order_ref[holder]] = slot
    lowest = BLOCKS
    for step in range(2):
        block = blocks[1 - step]
        row = block * BLOCK
        low = start_of(row)
        lowest = jnp.minimum(lowest, low // BLOCK)
        table_ref[TABLE_BLOCK + step] = block
        table_ref[TABLE_LOW + step] = low
        table_ref[TABLE_HIGH + step] = start_of(row + BLOCK - 1)
    table_ref[TABLE_RANGE] = lowest
    table_ref[TABLE_RANGE + 1] = jnp.maximum(blocks[0], blocks[1]) + 1
    table_ref[TABLE_CORE] = core


def plan(place, lengths, order, bias, inverse, bias_heads):
    vmem = pl.BlockSpec(memory_space=pltpu.VMEM)
    return pl.pallas_call(
        functools.partial(plan_kernel, bias_heads),
        grid_spec=pltpu.PrefetchScalarGridSpec(
            num_scalar_prefetch=3,
            grid=(1,),
            in_specs=[vmem] * 2,
            out_specs=[vmem] * 3 + [pl.BlockSpec(memory_space=pltpu.SMEM)],
        ),
        out_shape=[
            jax.ShapeDtypeStruct((2 * BLOCK, HEAD_DIM), jnp.float32),
            jax.ShapeDtypeStruct((2 * BLOCK, 1), jnp.int32),
            jax.ShapeDtypeStruct((1, len(bias_heads[0]) * HEAD_DIM), jnp.float32),
            jax.ShapeDtypeStruct((TABLE_CORE + 1,), jnp.int32),
        ],
        compiler_params=pltpu.CompilerParams(vmem_limit_bytes=VMEM),
    )(place, lengths, order, bias, inverse)


def body(hidden, w_qkv, bias_qkv, doc_lengths, span_order):
    x, core = lax.axis_index("x"), lax.axis_index("core")
    y, z = lax.axis_index("y"), lax.axis_index("z")
    place = jnp.stack([y, z, x, core]).astype(jnp.int32)

    heads = [[HEADS_Q + g, HEADS_Q + KV_HEADS + g] + [g * PER_KV + i for i in range(PER_KV)] for g in range(KV_HEADS)]
    heads_of = [heads[g][:2] + heads[1 - g][:2] + heads[g][2:] + heads[1 - g][2:] for g in range(KV_HEADS)]
    chunk = arrange(place, w_qkv, heads_of)
    kv, columns = 2 * HEAD_DIM, w_qkv.shape[1]
    chunks = around(chunk, lambda a, d: shift(a, "x", d))

    group = jnp.arange(GROUP, dtype=jnp.int32)
    in_slot = group % SLOT
    source = (
        (z + RING - (group % (GROUP // 2)) // SLOT) % RING * (2 * SLOT)
        + (x + RING - in_slot // CORE_ROWS) % RING * (2 * CORE_ROWS)
        + group // (GROUP // 2) * CORE_ROWS
        + in_slot % CORE_ROWS
    )
    own = permute_columns(place, source[None].astype(jnp.int32), after(hidden[0], chunk))
    slot = stack(chunks)
    slot, own, bias_qkv, doc_lengths, span_order = lax.optimization_barrier(
        (slot, own, bias_qkv, doc_lengths, span_order)
    )
    early = around(slot, lambda a, d: shift_by_core(a, EARLY, d))
    partner = swap_cores(own)

    half = HEAD_DIM // 2
    inverse = ROPE_BASE ** (-(jnp.arange(half).astype(jnp.float32) * 2.0) / HEAD_DIM)
    angles, start_column, bias, table = plan(
        place, doc_lengths[0], span_order[0], bias_qkv[None], jnp.concatenate([inverse, inverse])[None], heads
    )
    sign = jnp.where(jnp.arange(HEAD_DIM) < half, -1.0, 1.0)
    cosine, sine = jnp.cos(angles), jnp.sin(angles) * sign[None]
    early[0], bias, cosine, sine, table, start_column = lax.optimization_barrier(
        (early[0], bias, cosine, sine, table, start_column)
    )
    kv_block, q_block = place_rows(early, (0, 2 * kv, columns))
    kv_pieces = gather_direct(kv_block)
    q_block = after(q_block, *kv_pieces[0])
    q_near = gather_near(q_block)
    kv_terms = [(a, 0, d, 0, 0) for d, a in enumerate(kv_pieces[0])]
    kv_terms += [(a, 1, d, 0, kv) for d, a in enumerate(kv_pieces[1])]
    pairs = project(place, own, partner, kv_terms, kv, ends=(bias[:, :kv], cosine, sine), rotated=1)
    first, third = shift(pairs, "x", 1), shift(pairs, "x", -1)
    far = shift(first[:, :HEAD_DIM], "x", 1), shift(third[:, HEAD_DIM:], "x", -1)
    all_pairs = [pairs, first, *far, third]

    n = PER_KV * HEAD_DIM
    q_first, q_third = lax.optimization_barrier((*q_near, first, third))[:2]
    q_mine, q_other = gather_far(q_first, q_third)
    near_other = jnp.concatenate([q_block[:, n:], q_first[:, n:], q_third[:, n:]], axis=0)
    near_other = swap_cores(near_other)
    near = [(q_block, 0, 0, 0, 0), (q_first, 0, 1, 0, 0), (q_third, 0, 3, 0, 0)]
    near += [(near_other, 1, d, i * (GROUP // 2), 0) for i, d in enumerate((0, 1, 3))]
    partial = project(place, own, partner, near, n)
    q_other, q_mine = lax.optimization_barrier((q_other, q_mine, partial, *far))[:2]
    last = [(q_mine, 0, 2, 0, 0), (swap_cores(q_other), 1, 2, 0, 0)]
    queries = project(place, own, partner, last, n, partial, (bias[:, kv:], cosine, sine), PER_KV)
    their_rows, result = attend(table, queries, start_column, all_pairs)
    at = (1 - core) * (PER_KV * HEAD_DIM)
    return lax.dynamic_update_slice(result, swap_cores(their_rows), (0, at))[None]


def solution(mesh):
    fine = Mesh(mesh.devices.reshape(RING, RING, RING, 2), ("y", "z", "x", "core"))
    rows = P(("y", "z"), ("x", "core"), None)
    in_specs = (rows, P(("y", "z", "x", "core"), None), P(), P(("y", "z"), None), P(("y", "z"), None))
    return jax.shard_map(body, mesh=fine, in_specs=in_specs, out_specs=rows, check_vma=False)
```
